128 devices in a mesh: slab: 32 (over z_lo, x, y), energy: 4 (over z_hi, core).
Axes of the slice: x: 4, y: 4, z: 4 (z_hi: 2, z_lo: 2; z = z_hi * 2 + z_lo), core: 2. Of those that a mesh axis runs over, the one named last changes fastest.
Arguments:
- onsite: float32 [32, 256, 256], P('slab'), may hold values from -1.4 to 0.3, as said below
- coupling: float32 [32, 256, 256], P('slab'), may hold values from -0.25 to 1.6
- pattern: int32 [32, 4, 4], P('slab'), may hold values 0 or 1
- contact_rates: float32 [2, 256], replicated, may hold values from 1 to 3
- energy_index: int32 [16], P('energy'), parts along dimension 0, may hold values from 0 to 31
Outputs:
- spectral: float32 [32, 16, 256], P('slab', 'energy'), parts along dimension 1
- transmission: float32 [16], P('energy'), parts along dimension 0
The draws below stay inside these ranges and needn't reach their ends.
There are 4 independent parts, one for each index of `energy`. The reference program is written for one: setup_inputs(seed, part) draws one part's arguments, and reference() takes and returns one part's arrays. A program takes and returns all parts, laid end to end along the dimension named above; an argument that names none is the same for every part. Nothing has to cross between parts.
Inputs may be any that keep to these rules, and one draw needn't show every extreme that they name: Every onsite block is symmetric.
All inputs are finite; a program needn't handle non-finite values. No bound on the sum of `pattern` on one device may be relied on, other than what follows from the above.
Results may differ from the reference program's by a relative error of at most 0.00012.
Values sent between devices are 32-bit elements; how exact they have to be, the bound alone decides.
No kernel may reach another device: no remote copies, remote signals or barrier semaphores. Data moves between devices by JAX's collectives and lax.ppermute only.
A program may use at most 64 MiB of HBM per device.

```python
import math
import jax
import jax.numpy as jnp
from jax import lax

W = 256
NT = 4
NE = 4
ITERS = 2
GRID = 32
NS = 32
MID = 16


def draw_onsite(key, part):
    key_offdiag, key_levels = jax.random.split(key)
    entries = jnp.clip(jax.random.normal(key_offdiag, (NS, W, W), jnp.float32), -6.0, 6.0) * (0.17 / math.sqrt(W))
    symmetric = (entries + jnp.swapaxes(entries, 1, 2)) * 0.70710678
    levels = jax.random.uniform(key_levels, (NS, W), jnp.float32, -1.4, -0.8)
    diagonal_mask = jnp.eye(W, dtype=bool)
    return jnp.where(diagonal_mask[None, :, :], levels[:, None, :], symmetric)


def draw_coupling(key, part):
    key_strength, key_rest = jax.random.split(jax.random.fold_in(key, 17))
    strengths = jax.random.uniform(key_strength, (NS, W), jnp.float32, 1.3, 1.6)
    rest = jnp.clip(jax.random.normal(key_rest, (NS, W, W), jnp.float32), -6.0, 6.0) * (0.11 / math.sqrt(W))
    diagonal_mask = jnp.eye(W, dtype=bool)
    return jnp.where(diagonal_mask[None, :, :], strengths[:, None, :], rest)


def set_ends(array, rng, least, top_value):
    index_at = [jax.random.randint(jax.random.fold_in(rng, axis), (), 0, length) for axis, length in enumerate(array.shape)]
    main_axis = array.shape.index(max(array.shape))
    neighbour = index_at[:main_axis] + [(index_at[main_axis] + 1) % array.shape[main_axis]] + index_at[main_axis + 1:]
    return array.at[tuple(index_at)].set(least).at[tuple(neighbour)].set(top_value)


def setup_inputs(seed: int = 0, part: int = 0) -> dict:
    arg_keys = jax.random.split(jax.random.key(seed), 6)
    own_keys = jax.random.split(jax.random.fold_in(arg_keys[5], part), 6)
    onsite = draw_onsite(jax.random.fold_in(arg_keys[5], 71), part)
    coupling = draw_coupling(jax.random.fold_in(arg_keys[5], 71), part)
    pattern = set_ends((jax.random.randint(arg_keys[2], (NS, NT, NT), 0, 8) < 7).astype(jnp.int32), jax.random.fold_in(arg_keys[2], 1), 0, 1)
    contact_rates = jnp.clip(jnp.exp(jax.random.uniform(arg_keys[3], (2, W), jnp.float32, math.log(1.0), math.log(3.0))), 1.0, 3.0)
    energy_index = set_ends(jax.random.randint(own_keys[4], (NE,), 0, GRID), jax.random.fold_in(own_keys[4], 1), 0, GRID - 1).astype(jnp.int32)
    return dict(onsite=onsite, coupling=coupling, pattern=pattern, contact_rates=contact_rates, energy_index=energy_index)


energy_floor = -0.2
energy_spacing = 0.0125
broadening = 0.3
highest = lax.Precision.HIGHEST


def product(left_factor, right_factor):
    return jnp.dot(left_factor, right_factor, preferred_element_type=jnp.float32, precision=highest)


def complex_product(left_factor, right_factor):
    real_real = product(left_factor[0], right_factor[0])
    imag_imag = product(left_factor[1], right_factor[1])
    summed = product(left_factor[0] + left_factor[1], right_factor[0] + right_factor[1])
    return jnp.stack([real_real - imag_imag, summed - real_real - imag_imag])


def schur_after(coupling_block, greens):
    halfway = jnp.stack([product(greens[0], coupling_block), product(greens[1], coupling_block)])
    transposed = coupling_block.T
    return jnp.stack([product(transposed, halfway[0]), product(transposed, halfway[1])])


def schur_before(coupling_block, greens):
    transposed = coupling_block.T
    halfway = jnp.stack([product(greens[0], transposed), product(greens[1], transposed)])
    return jnp.stack([product(coupling_block, halfway[0]), product(coupling_block, halfway[1])])


def invert(matrix):
    orbitals = matrix.shape[1]
    diag_real = jnp.diagonal(matrix[0])
    diag_imag = jnp.diagonal(matrix[1])
    modulus = diag_real * diag_real + diag_imag * diag_imag
    start_real = diag_real / modulus
    start_imag = -diag_imag / modulus
    identity = jnp.eye(orbitals, dtype=jnp.float32)
    applied_real = matrix[0] * start_real[None, :] - matrix[1] * start_imag[None, :]
    applied_imag = matrix[0] * start_imag[None, :] + matrix[1] * start_real[None, :]
    scaled_real = start_real[:, None] * applied_real - start_imag[:, None] * applied_imag
    scaled_imag = start_real[:, None] * applied_imag + start_imag[:, None] * applied_real
    approx = jnp.stack([2.0 * identity * start_real[None, :] - scaled_real,
                        2.0 * identity * start_imag[None, :] - scaled_imag])
    for iteration in range(ITERS - 1):
        applied = complex_product(matrix, approx)
        approx = 2.0 * approx - complex_product(approx, applied)
    return approx


def green_block(energy, onsite_block, self_energy):
    identity = jnp.eye(onsite_block.shape[0], dtype=jnp.float32)
    real_part = energy * identity - onsite_block - self_energy[0]
    imag_part = broadening * identity - self_energy[1]
    return invert(jnp.stack([real_part, imag_part]))


def spectral_row(greens):
    return -2.0 * jnp.diagonal(greens[1])


def transmitted(left_energy, right_energy, greens):
    gamma_left = -2.0 * left_energy[1]
    gamma_right = -2.0 * right_energy[1]
    forward_real = product(gamma_left, greens[0])
    forward_imag = product(gamma_left, greens[1])
    backward_real = product(gamma_right, greens[0].T)
    backward_imag = -product(gamma_right, greens[1].T)
    return jnp.sum(forward_real * backward_real.T) - jnp.sum(forward_imag * backward_imag.T)


def contact_energy(rates):
    identity = jnp.eye(rates.shape[0], dtype=jnp.float32)
    return jnp.stack([jnp.zeros_like(identity), identity * (-0.5 * rates)[None, :]])


def mask_coupling(coupling, pattern):
    slab_count = coupling.shape[0]
    orbitals = coupling.shape[1]
    tile_count = pattern.shape[1]
    tile_size = orbitals // tile_count
    blocks = coupling.reshape(slab_count, tile_count, tile_size, tile_count, tile_size)
    blocks = blocks * pattern.astype(jnp.float32)[:, :, None, :, None]
    return blocks.reshape(slab_count, orbitals, orbitals)


def reference(onsite, coupling, pattern, contact_rates, energy_index):
    masked = mask_coupling(coupling, pattern)
    energies = energy_floor + energy_spacing * energy_index.astype(jnp.float32)
    left_contact = contact_energy(contact_rates[0])
    right_contact = contact_energy(contact_rates[1])

    def one_energy(energy):
        def left_step(carried, pieces):
            greens = green_block(energy, pieces[0], carried)
            return schur_after(pieces[1], greens), carried

        def right_step(carried, pieces):
            greens = green_block(energy, pieces[0], carried)
            return schur_before(pieces[1], greens), carried

        unused, lefts = lax.scan(left_step, left_contact, (onsite[:NS - 1], masked[:NS - 1]))
        last_left = schur_after(masked[NS - 2], green_block(energy, onsite[NS - 2], lefts[NS - 2]))
        lefts = jnp.concatenate([lefts, last_left[None]], axis=0)
        lowest, uppers = lax.scan(right_step, right_contact, (onsite[1:][::-1], masked[:NS - 1][::-1]))
        rights = jnp.concatenate([lowest[None], uppers[::-1]], axis=0)

        def slab_spectrum(pieces):
            return spectral_row(green_block(energy, pieces[0], pieces[1] + pieces[2]))

        spectra = lax.map(slab_spectrum, (onsite, lefts, rights))
        middle = green_block(energy, onsite[MID], lefts[MID] + rights[MID])
        return spectra, transmitted(lefts[MID], rights[MID], middle)

    spectra, crossing = lax.map(one_energy, energies)
    return jnp.transpose(spectra, (1, 0, 2)), crossing
```

```python
import functools
import jax
import jax.numpy as jnp
from jax import lax
from jax.experimental import pallas as pl
from jax.experimental.pallas import tpu as pltpu
from jax.sharding import Mesh
from jax.sharding import PartitionSpec as P

energy_floor = -0.2
energy_spacing = 0.0125
broadening = 0.3
W = 256
f32 = jnp.float32
b16 = jnp.bfloat16
VMEM_BYTES = 56 * 2**20


def dot_nt(left, right):
    return lax.dot_general(left, right, (((1,), (1,)), ((), ())), preferred_element_type=f32)


def dot_nn(left, right):
    return lax.dot_general(left, right, (((1,), (0,)), ((), ())), preferred_element_type=f32)


def split(value):
    high = value.astype(b16)
    return high, (value - high.astype(f32)).astype(b16)


def dot3(left, right, dot=dot_nt):
    return dot(left[0], right[0]) + (dot(left[1], right[0]) + dot(left[0], right[1]))


def cdot3(left, right, dot=dot_nt):
    (lr, li), (rr, ri) = left, right
    first = dot3(split(lr), split(rr), dot)
    second = dot3(split(li), split(ri), dot)
    summed = dot3(split(lr + li), split(rr + ri), dot)
    return first - second, summed - first - second


def eye_mask():
    rows = lax.broadcasted_iota(jnp.int32, (W, W), 0)
    columns = lax.broadcasted_iota(jnp.int32, (W, W), 1)
    return rows == columns


def diagonal_row(value):
    return jnp.sum(jnp.where(eye_mask(), value, 0.0), axis=0, keepdims=True)


def diagonal_and_rest(energy, onsite, sr, si):
    br = -(onsite + sr)
    bi = -si
    dr = energy + diagonal_row(br)
    di = broadening + diagonal_row(bi)
    scale = 1.0 / (dr * dr + di * di)
    dr, di = dr * scale, -di * scale
    mask = eye_mask()
    br = jnp.where(mask, 0.0, br)
    bi = jnp.where(mask, 0.0, bi)
    return br, bi, dr, di, br * dr - bi * di, br * di + bi * dr


def chain_step(energy, onsite, lead, sr, si):
    _, _, dr, di, fr, fi = diagonal_and_rest(energy, onsite, sr, si)
    frs, fis, leads = split(fr), split(fi), split(lead)
    pr, pi = dot3(leads, frs), dot3(leads, fis)
    prh, pih = pr.astype(b16), pi.astype(b16)
    qr = dot_nt(prh, frs[0]) - dot_nt(pih, fis[0])
    qi = dot_nt(prh, fis[0]) + dot_nt(pih, frs[0])
    x = lead - pr
    xr, xi = x * dr + pi * di, x * di - pi * dr
    return cdot3((xr, xi), (lead + qr, qi))


def spectral_row(energy, onsite, sr, si):
    br, bi, dr, di, fr, fi = diagonal_and_rest(energy, onsite, sr, si)
    frh, fih, brh, bih = (v.astype(b16) for v in (fr, fi, br, bi))
    yr = br - (dot_nt(frh, brh) - dot_nt(fih, bih))
    yi = bi - (dot_nt(frh, bih) + dot_nt(fih, brh))
    tr = jnp.sum(fr * yr - fi * yi, axis=1, keepdims=True)
    ti = jnp.sum(fr * yi + fi * yr, axis=1, keepdims=True)
    tr = diagonal_row(jnp.broadcast_to(tr, (W, W)))
    ti = diagonal_row(jnp.broadcast_to(ti, (W, W)))
    return -2.0 * (di + (dr * dr - di * di) * ti + 2.0 * dr * di * tr)


def crossing_row(energy, onsite, s0, s1, r0, r1):
    br, bi, dr, di, fr, fi = diagonal_and_rest(energy, onsite, s0 + r0, s1 + r1)
    f2r, f2i = cdot3((fr, fi), (fr, fi), dot_nn)
    f3r, f3i = cdot3((f2r, f2i), (fr, fi), dot_nn)
    one = jnp.where(eye_mask(), 1.0, 0.0)
    kr, ki = one - fr + f2r - f3r, -fi + f2i - f3i
    dcol_r = jnp.where(eye_mask(), dr, 0.0)
    dcol_i = jnp.where(eye_mask(), di, 0.0)
    dcol_r = jnp.sum(dcol_r, axis=1, keepdims=True)
    dcol_i = jnp.sum(dcol_i, axis=1, keepdims=True)
    gr, gi = dcol_r * kr - dcol_i * ki, dcol_r * ki + dcol_i * kr
    left, right = split(-2.0 * s1), split(-2.0 * r1)
    grs, gis = split(gr), split(gi)
    ar, ai = dot3(left, grs, dot_nn), dot3(left, gis, dot_nn)
    cr, ci = dot3(grs, right, dot_nt), dot3(gis, right, dot_nt)
    return jnp.sum(ar * cr + ai * ci, axis=0, keepdims=True)


def first_kernel(steps, place, energy, rates, wire, store, last, hbuf, mbuf, sbuf, in_sem, out_sem):
    flip = place[0]

    def fetch(t):
        slab = jnp.where(flip == 0, t, 15 - t)
        link = jnp.where(flip == 0, t, 14 - t)
        return (
            pltpu.make_async_copy(wire.at[slab, 0], hbuf.at[t], in_sem.at[t, 0]),
            pltpu.make_async_copy(wire.at[link, 1], mbuf.at[t], in_sem.at[t, 1]),
        )

    for t in range(steps):
        for copy in fetch(t):
            copy.start()
    sbuf[0, 0] = jnp.zeros((W, W), f32)
    sbuf[0, 1] = jnp.where(eye_mask(), -0.5 * rates[...], 0.0)

    def body(t, unused):
        for copy in fetch(t):
            copy.wait()
        pltpu.make_async_copy(sbuf.at[t], store.at[t], out_sem.at[t]).start()
        m = mbuf[t]
        lead = jnp.where(flip == 0, m.T, m)
        nr, ni = chain_step(energy[0], hbuf[t], lead, sbuf[t, 0], sbuf[t, 1])
        sbuf[t + 1, 0] = nr
        sbuf[t + 1, 1] = ni
        return 0

    lax.fori_loop(0, steps, body, 0)
    last[...] = sbuf[steps]
    for t in range(steps):
        pltpu.make_async_copy(sbuf.at[t], store.at[t], out_sem.at[t]).wait()


def edge_kernel(place, energy, onsite, link, entering, leaving):
    m = link[...]
    lead = jnp.where(place[0] == 0, m.T, m)
    nr, ni = chain_step(energy[0], onsite[...], lead, entering[0], entering[1])
    leaving[0] = nr
    leaving[1] = ni


def second_kernel(place, energy, wire, store, edge, arrived, spectra, crossing, hbuf, mbuf, sbuf, carried, in_sem):
    flip = place[0]

    def fetch(t):
        slab = jnp.where(flip == 0, 15 - t, t)
        link = jnp.where(flip == 0, jnp.maximum(14 - t, 0), t)
        return (
            pltpu.make_async_copy(wire.at[slab, 0], hbuf.at[t], in_sem.at[t, 0]),
            pltpu.make_async_copy(wire.at[link, 1], mbuf.at[t], in_sem.at[t, 1]),
        )

    def stored(t):
        return pltpu.make_async_copy(store.at[15 - t], sbuf.at[t], in_sem.at[t, 2])

    for t in range(16):
        for copy in fetch(t):
            copy.start()
        if t:
            stored(t).start()
    carried[...] = arrived[...]
    sbuf[0] = edge[...]
    crossing[...] = jnp.zeros((1, W), f32)

    def spectrum(t):
        row = spectral_row(energy[0], hbuf[t], sbuf[t, 0] + carried[0], sbuf[t, 1] + carried[1])
        slab = jnp.where(flip == 0, 15 - t, t)
        spectra[pl.ds(slab, 1)] = row[None]

    def advance(t):
        m = mbuf[t]
        lead = jnp.where(flip == 0, m, m.T)
        nr, ni = chain_step(energy[0], hbuf[t], lead, carried[0], carried[1])
        carried[0] = nr
        carried[1] = ni

    for copy in fetch(0):
        copy.wait()

    @pl.when(flip != 0)
    def _():
        crossing[...] = crossing_row(energy[0], hbuf[0], carried[0], carried[1], sbuf[0, 0], sbuf[0, 1])

    spectrum(0)
    advance(0)

    def body(t, unused):
        for copy in fetch(t):
            copy.wait()
        stored(t).wait()
        spectrum(t)
        advance(t)
        return 0

    lax.fori_loop(1, 15, body, 0)
    for copy in fetch(15):
        copy.wait()
    stored(15).wait()
    spectrum(15)


def vmem():
    return pl.BlockSpec(memory_space=pltpu.VMEM)


def smem():
    return pl.BlockSpec(memory_space=pltpu.SMEM)


def anywhere():
    return pl.BlockSpec(memory_space=pl.ANY)


def params():
    return pltpu.CompilerParams(vmem_limit_bytes=VMEM_BYTES)


def first_sweep(place, energy, rates, wire):
    steps = 15
    return pl.pallas_call(
        functools.partial(first_kernel, steps),
        out_shape=(jax.ShapeDtypeStruct((steps, 2, W, W), f32), jax.ShapeDtypeStruct((2, W, W), f32)),
        in_specs=[smem(), smem(), vmem(), anywhere()],
        out_specs=[anywhere(), vmem()],
        scratch_shapes=[
            pltpu.VMEM((steps, W, W), f32),
            pltpu.VMEM((steps, W, W), f32),
            pltpu.VMEM((steps + 1, 2, W, W), f32),
            pltpu.SemaphoreType.DMA((steps, 2)),
            pltpu.SemaphoreType.DMA((steps,)),
        ],
        name="first_sweep",
        compiler_params=params(),
        cost_estimate=pl.CostEstimate(flops=15 * 20 * 2 * W**3, bytes_accessed=15 * 2**20, transcendentals=0),
    )(place, energy, rates, wire)


def edge_step(place, energy, onsite, link, entering):
    return pl.pallas_call(
        edge_kernel,
        out_shape=jax.ShapeDtypeStruct((2, W, W), f32),
        in_specs=[smem(), smem(), vmem(), vmem(), vmem()],
        out_specs=vmem(),
        name="edge_step",
        compiler_params=params(),
    )(place, energy, onsite, link, entering)


def second_sweep(place, energy, wire, store, edge, arrived):
    return pl.pallas_call(
        second_kernel,
        out_shape=(jax.ShapeDtypeStruct((16, 1, W), f32), jax.ShapeDtypeStruct((1, W), f32)),
        in_specs=[smem(), smem(), anywhere(), anywhere(), vmem(), vmem()],
        out_specs=[vmem(), vmem()],
        scratch_shapes=[
            pltpu.VMEM((16, W, W), f32),
            pltpu.VMEM((16, W, W), f32),
            pltpu.VMEM((16, 2, W, W), f32),
            pltpu.VMEM((2, W, W), f32),
            pltpu.SemaphoreType.DMA((16, 3)),
        ],
        name="second_sweep",
        compiler_params=params(),
    )(place, energy, wire, store, edge, arrived)


def on_device(onsite, coupling, pattern, contact_rates, energy_index):
    half, x, y, core = (lax.axis_index(name) for name in ("half", "x", "y", "core"))
    mask = jnp.repeat(jnp.repeat(pattern[0].astype(f32), 64, axis=0), 64, axis=1)
    masked = coupling[0] * mask
    wire = lax.all_gather(jnp.where(core == 0, onsite[0], masked), ("x", "y", "core"), tiled=False)
    wire = wire.reshape(16, 2, W, W)
    place = half.astype(jnp.int32)[None]
    energies = energy_floor + energy_spacing * energy_index.astype(f32)
    energy = lax.dynamic_slice(energies, (y,), (1,))
    rates = lax.dynamic_slice(contact_rates, (half, 0), (1, W))

    bridge = lax.ppermute(wire[15, 1], "half", [(0, 1)])
    bridge = jnp.where(half == 0, wire[15, 1], bridge)
    inner = lax.dynamic_index_in_dim(wire[:, 0], jnp.where(half == 0, 15, 0), 0, keepdims=False)
    store, edge = first_sweep(place, energy, rates, wire)
    leaving = edge_step(place, energy, inner, bridge, edge)
    arrived = lax.ppermute(leaving, "half", [(0, 1), (1, 0)])
    spectra, crossing = second_sweep(place, energy, wire, store, edge, arrived)

    total = jnp.broadcast_to(jnp.sum(crossing), (1, W))
    mine = jnp.concatenate([lax.dynamic_slice(spectra[:, 0], (4 * x, 0), (4, W)), total], axis=0)

    def sent(shift):
        row = lax.dynamic_slice(mine, (lax.rem(y + shift, 4), 0), (1, W))
        return jnp.concatenate([row, total], axis=0)

    pieces = [sent(0)]
    for shift in (1, 2, 3):
        pieces.append(lax.ppermute(sent(shift), "y", [(a, (a + shift) % 4) for a in range(4)]))
    turned = jnp.stack((pieces[::-1]) * 2)
    gathered = lax.dynamic_slice(turned, (3 - y, 0, 0), (4, 2, W))
    spectral = gathered[:, 0]
    totals = gathered[:, 1]
    totals = jnp.where(half == 0, lax.ppermute(totals, "half", [(1, 0)]), totals)
    return spectral[None], totals[:, 0]


def solution(mesh):
    fine = Mesh(mesh.devices.reshape(2, 4, 4, 2, 2), ("half", "x", "y", "plane", "core"))
    slab = ("half", "x", "y")
    part = ("plane", "core")
    return jax.shard_map(
        on_device,
        mesh=fine,
        in_specs=(P(slab), P(slab), P(slab), P(), P(part)),
        out_specs=(P(slab, part, None), P(part)),
        check_vma=False,
    )
```

```python
import functools
import jax
import jax.numpy as jnp
from jax import lax
from jax.experimental import pallas as pl
from jax.experimental.pallas import tpu as pltpu
from jax.sharding import Mesh
from jax.sharding import PartitionSpec as P

energy_floor = -0.2
energy_spacing = 0.0125
broadening = 0.3
W = 256
f32 = jnp.float32
b16 = jnp.bfloat16
VMEM_BYTES = 32 * 2**20


def dot_nt(left, right):
    return lax.dot_general(left, right, (((1,), (1,)), ((), ())), preferred_element_type=f32)


def dot_nn(left, right):
    return lax.dot_general(left, right, (((1,), (0,)), ((), ())), preferred_element_type=f32)


def split(value):
    high = value.astype(b16)
    return high, (value - high.astype(f32)).astype(b16)


def dot3(left, right, dot=dot_nt):
    return dot(left[0], right[0]) + (dot(left[1], right[0]) + dot(left[0], right[1]))


def cdot3(left, right, dot=dot_nt):
    (lr, li), (rr, ri) = left, right
    first = dot3(split(lr), split(rr), dot)
    second = dot3(split(li), split(ri), dot)
    summed = dot3(split(lr + li), split(rr + ri), dot)
    return first - second, summed - first - second


def eye_mask():
    rows = lax.broadcasted_iota(jnp.int32, (W, W), 0)
    columns = lax.broadcasted_iota(jnp.int32, (W, W), 1)
    return rows == columns


def diagonal_row(value):
    return jnp.sum(jnp.where(eye_mask(), value, 0.0), axis=0, keepdims=True)


def diagonal_and_rest(energy, onsite, sr, si):
    br = -(onsite + sr)
    bi = -si
    dr = energy + diagonal_row(br)
    di = broadening + diagonal_row(bi)
    scale = 1.0 / (dr * dr + di * di)
    dr, di = dr * scale, -di * scale
    mask = eye_mask()
    br = jnp.where(mask, 0.0, br)
    bi = jnp.where(mask, 0.0, bi)
    return br, bi, dr, di, br * dr - bi * di, br * di + bi * dr


def chain_step(energy, onsite, lead, sr, si):
    _, _, dr, di, fr, fi = diagonal_and_rest(energy, onsite, sr, si)
    frs, fis, leads = split(fr), split(fi), split(lead)
    pr, pi = dot3(leads, frs), dot3(leads, fis)
    prh, pih = pr.astype(b16), pi.astype(b16)
    qr = dot_nt(prh, frs[0]) - dot_nt(pih, fis[0])
    qi = dot_nt(prh, fis[0]) + dot_nt(pih, frs[0])
    x = lead - pr
    xr, xi = x * dr + pi * di, x * di - pi * dr
    return cdot3((xr, xi), (lead + qr, qi))


def spectral_row(energy, onsite, sr, si):
    br, bi, dr, di, fr, fi = diagonal_and_rest(energy, onsite, sr, si)
    frh, fih, brh, bih = (v.astype(b16) for v in (fr, fi, br, bi))
    yr = br - (dot_nt(frh, brh) - dot_nt(fih, bih))
    yi = bi - (dot_nt(frh, bih) + dot_nt(fih, brh))
    tr = jnp.sum(fr * yr - fi * yi, axis=1, keepdims=True)
    ti = jnp.sum(fr * yi + fi * yr, axis=1, keepdims=True)
    tr = diagonal_row(jnp.broadcast_to(tr, (W, W)))
    ti = diagonal_row(jnp.broadcast_to(ti, (W, W)))
    return -2.0 * (di + (dr * dr - di * di) * ti + 2.0 * dr * di * tr)


def crossing_row(energy, onsite, s0, s1, r0, r1):
    br, bi, dr, di, fr, fi = diagonal_and_rest(energy, onsite, s0 + r0, s1 + r1)
    f2r, f2i = cdot3((fr, fi), (fr, fi), dot_nn)
    f3r, f3i = cdot3((f2r, f2i), (fr, fi), dot_nn)
    one = jnp.where(eye_mask(), 1.0, 0.0)
    kr, ki = one - fr + f2r - f3r, -fi + f2i - f3i
    dcol_r = jnp.where(eye_mask(), dr, 0.0)
    dcol_i = jnp.where(eye_mask(), di, 0.0)
    dcol_r = jnp.sum(dcol_r, axis=1, keepdims=True)
    dcol_i = jnp.sum(dcol_i, axis=1, keepdims=True)
    gr, gi = dcol_r * kr - dcol_i * ki, dcol_r * ki + dcol_i * kr
    left, right = split(-2.0 * s1), split(-2.0 * r1)
    grs, gis = split(gr), split(gi)
    ar, ai = dot3(left, grs, dot_nn), dot3(left, gis, dot_nn)
    cr, ci = dot3(grs, right, dot_nt), dot3(gis, right, dot_nt)
    return jnp.sum(ar * cr + ai * ci, axis=0, keepdims=True)


H2 = W // 2


def here(name):
    return lax.axis_index(name)


def on_task():
    x = here("x")
    return ((x == 0) | (x == 3)) == (here("core") == 0)


def is_outer():
    return (here("x") < 2) == (here("half") == 0)


def pack(sr, si, extra=0.0):
    rows = lax.broadcasted_iota(jnp.int32, (H2, H2), 0)
    columns = lax.broadcasted_iota(jnp.int32, (H2, H2), 1)

    def folded(value):
        low = value[H2:, H2:]
        fold = jnp.where(rows <= columns, value[:H2, :H2], low)
        diagonal = jnp.sum(jnp.where(rows == columns, low, 0.0), axis=0, keepdims=True)
        return jnp.concatenate([value[:H2, H2:], fold], axis=1), diagonal

    top, diagonal_top = folded(sr)
    bottom, diagonal_bottom = folded(si)
    row = jnp.broadcast_to(jnp.concatenate([diagonal_top, diagonal_bottom], axis=1), (8, W))
    last = jnp.where(lax.broadcasted_iota(jnp.int32, (8, W), 0) == 0, row, extra)
    return jnp.concatenate([top, bottom, last], axis=0)


def unpack(packed):
    rows = lax.broadcasted_iota(jnp.int32, (H2, H2), 0)
    columns = lax.broadcasted_iota(jnp.int32, (H2, H2), 1)

    def unfolded(value, diagonal):
        corner, fold = value[:, :H2], value[:, H2:]
        turned = fold.T
        first = jnp.where(rows <= columns, fold, turned)
        last = jnp.where(rows > columns, fold, jnp.where(rows < columns, turned, diagonal))
        top = jnp.concatenate([first, corner], axis=1)
        return jnp.concatenate([top, jnp.concatenate([corner.T, last], axis=1)], axis=0)

    return (
        unfolded(packed[:H2], packed[2 * H2 : 2 * H2 + 1, :H2]),
        unfolded(packed[H2 : 2 * H2], packed[2 * H2 : 2 * H2 + 1, H2:]),
    )


def prepare_kernel(pattern, onsite, coupling, both, mine):
    tiles = lax.broadcasted_iota(jnp.int32, (1, W), 1) // 64
    both[0] = onsite[...]
    for p in range(4):
        row = jnp.zeros((1, W), f32)
        for q in range(4):
            row = jnp.where(tiles == q, pattern[p, q].astype(f32), row)
        part = pl.ds(64 * p, 64)
        both[1, part, :] = coupling[part, :] * row
    mine[...] = both[here("core")]


def energy_of(index):
    return energy_floor + energy_spacing * index[here("y")].astype(f32)


STEPS = ((0, 3), (3, 7), (7, 8), (8, 16))
OUTWARD = ((1, 4), (4, 8), (8, 16))


def kept_at(t):
    part = next(k for k, (first, stop) in enumerate(STEPS) if first <= t < stop)
    return part, t - STEPS[part][0]


def sweep_kernel(part, *refs):
    first, stop = STEPS[part]
    count = stop - first
    refs = list(refs)
    index = refs.pop(0)
    start = refs.pop(0)
    both, own_mine, own_sent, near_mine, near_sent = (refs.pop(0) for _ in range(5))
    bridge = refs.pop(0) if part > 1 else None
    wire_h, wire_m, store, last = (refs.pop(0) for _ in range(4))
    hbuf, mbuf, sbuf, in_sem, out_sem = refs
    half, y, core = here("half"), here("y"), here("core")
    energy = energy_of(index)

    def start_from(chunk, column, kind, target, sem):
        away = lax.rem(column - y + 4, 4)
        own_row = core == (0 if chunk in (0, 3) else 1)

        @pl.when(own_row & (away == 0))
        def _():
            pltpu.make_async_copy(both.at[kind], target, sem).start()

        for here_too, own, near in ((core == kind, own_mine, near_mine), (core != kind, own_sent, near_sent)):

            @pl.when(own_row & (away != 0) & here_too)
            def _():
                pltpu.make_async_copy(own.at[jnp.maximum(away - 1, 0)], target, sem).start()

            @pl.when(~own_row & here_too)
            def _():
                pltpu.make_async_copy(near.at[away], target, sem).start()

    @pl.when(on_task() & (is_outer() if part < 3 else ~is_outer()))
    def _():
        for n in range(count):
            t = first + n
            start_from(t // 4, jnp.where(half == 0, t % 4, 3 - t % 4), 0, hbuf.at[n], in_sem.at[n, 0])
            if t % 4 < 3:
                start_from(t // 4, jnp.where(half == 0, t % 4, 2 - t % 4), 1, mbuf.at[n], in_sem.at[n, 1])
            else:

                @pl.when(half == 0)
                def _():
                    start_from(t // 4, 3, 1, mbuf.at[n], in_sem.at[n, 1])

                @pl.when(half != 0)
                def _():
                    if t % 8 == 7:
                        pltpu.make_async_copy(bridge, mbuf.at[n], in_sem.at[n, 1]).start()
                    else:
                        start_from(t // 4 + 1, 3, 1, mbuf.at[n], in_sem.at[n, 1])

        if part == 0:
            sbuf[0, 0] = jnp.zeros((W, W), f32)
            sbuf[0, 1] = jnp.where(eye_mask(), -0.5 * start[pl.ds(half, 1), :], 0.0)
        elif part < 3:
            sbuf[0] = start[...]
        else:
            sbuf[0, 0], sbuf[0, 1] = unpack(start[...])

        def kept(n):
            return (
                pltpu.make_async_copy(hbuf.at[n], wire_h.at[n], out_sem.at[n, 0]),
                pltpu.make_async_copy(mbuf.at[n], wire_m.at[n], out_sem.at[n, 1]),
                pltpu.make_async_copy(sbuf.at[n], store.at[n], out_sem.at[n, 2]),
            )

        def one(n, unused):
            pltpu.make_async_copy(wire_h.at[n], hbuf.at[n], in_sem.at[n, 0]).wait()
            pltpu.make_async_copy(wire_m.at[n], mbuf.at[n], in_sem.at[n, 1]).wait()
            for copy in kept(n):
                copy.start()
            m = mbuf[n]
            lead = jnp.where(half == 0, m.T, m)
            nr, ni = chain_step(energy, hbuf[n], lead, sbuf[n, 0], sbuf[n, 1])
            sbuf[n + 1, 0] = nr
            sbuf[n + 1, 1] = ni
            return 0

        lax.fori_loop(0, count, one, 0)
        if part > 1:
            last[...] = pack(sbuf[count, 0], sbuf[count, 1])
        else:
            last[...] = sbuf[count]
        for n in range(count):
            for copy in kept(n):
                copy.wait()


def middle_kernel(index, arrived, wire_h, wire_m, store, carried, crossing, spectrum, hbuf, mbuf, sbuf, in_sem):
    half = here("half")
    energy = energy_of(index)
    crossing[...] = jnp.zeros((8, W), f32)

    @pl.when(on_task() & ~is_outer())
    def _():
        copies = (
            pltpu.make_async_copy(wire_h.at[kept_at(15)[1]], hbuf, in_sem.at[0]),
            pltpu.make_async_copy(wire_m.at[kept_at(14)[1]], mbuf, in_sem.at[1]),
            pltpu.make_async_copy(store.at[kept_at(15)[1]], sbuf, in_sem.at[2]),
        )
        for copy in copies:
            copy.start()
        sr, si = unpack(arrived[...])
        for copy in copies:
            copy.wait()

        @pl.when(half != 0)
        def _():
            row = crossing_row(energy, hbuf[...], sr, si, sbuf[0], sbuf[1])
            crossing[...] = jnp.broadcast_to(jnp.sum(row, axis=1, keepdims=True), (8, W))

        spectrum[...] = spectral_row(energy, hbuf[...], sbuf[0] + sr, sbuf[1] + si)
        m = mbuf[...]
        lead = jnp.where(half == 0, m, m.T)
        nr, ni = chain_step(energy, hbuf[...], lead, sr, si)
        carried[0] = nr
        carried[1] = ni


def outward_kernel(leg, places, *refs):
    first, stop = OUTWARD[leg]
    count = stop - first
    refs = list(refs)
    index = refs.pop(0)
    start = refs.pop(0)
    earlier = refs.pop(0)
    totals = [refs.pop(0) for _ in range(2)] if leg else None
    links = [refs.pop(0) for _ in range(2)] if leg == 1 else None
    kept = {place: refs.pop(0) for place in places}
    outs = [refs.pop(0) for _ in range(4 if leg == 2 else 2)]
    hbuf, mbuf, sbuf, carried, spectra, in_sem = refs
    half, x, y = here("half"), here("x"), here("y")
    energy = energy_of(index)

    @pl.when(on_task() & (is_outer() if leg == 2 else ~is_outer()))
    def _():
        for n in range(count):
            t = first + n
            k, at_n = kept_at(15 - t)
            pltpu.make_async_copy(kept[0, k].at[at_n], hbuf.at[n], in_sem.at[n, 0]).start()
            pltpu.make_async_copy(kept[2, k].at[at_n], sbuf.at[n], in_sem.at[n, 2]).start()
            if t == 7:
                for side in range(2):

                    @pl.when(half == side)
                    def _():
                        pltpu.make_async_copy(links[side], mbuf.at[n], in_sem.at[n, 1]).start()

            elif t < 15:
                k, at_n = kept_at(14 - t)
                pltpu.make_async_copy(kept[1, k].at[at_n], mbuf.at[n], in_sem.at[n, 1]).start()
        if leg == 2:
            carried[0], carried[1] = unpack(start[...])
        else:
            carried[...] = start[...]
        if leg == 0:
            spectra[pl.ds(jnp.where(half == 0, 15, 0), 1)] = earlier[...][None]
        elif leg == 1:
            spectra[...] = earlier[...]

        def landed(n, link=True):
            pltpu.make_async_copy(hbuf.at[n], hbuf.at[n], in_sem.at[n, 0]).wait()
            pltpu.make_async_copy(sbuf.at[n], sbuf.at[n], in_sem.at[n, 2]).wait()
            if link:
                pltpu.make_async_copy(mbuf.at[n], mbuf.at[n], in_sem.at[n, 1]).wait()

        def spectrum(n):
            row = spectral_row(energy, hbuf[n], sbuf[n, 0] + carried[0], sbuf[n, 1] + carried[1])
            spectra[pl.ds(jnp.where(half == 0, 15 - first - n, first + n), 1)] = row[None]

        def one(n, unused):
            landed(n)
            spectrum(n)
            m = mbuf[n]
            lead = jnp.where(half == 0, m, m.T)
            nr, ni = chain_step(energy, hbuf[n], lead, carried[0], carried[1])
            carried[0] = nr
            carried[1] = ni
            return 0

        lax.fori_loop(0, count - (leg == 2), one, 0)
        if leg == 2:
            landed(count - 1, False)
            spectrum(count - 1)
        elif leg == 1:
            outs[0][...] = pack(carried[0], carried[1], totals[0][...] + totals[1][...])
            outs[1][...] = spectra[...]
        else:
            outs[0][...] = carried[...]
            outs[1][...] = spectra[...]

    if leg == 2:

        @pl.when(on_task())
        def _():
            @pl.when(~is_outer())
            def _():
                spectra[...] = earlier[...]

            outer_total = start[pl.ds(2 * H2, 8), :]
            total = jnp.where(is_outer(), outer_total, totals[0][...] + totals[1][...])
            partner = x + 1 - 2 * lax.rem(x, 2)
            for shift in range(4):
                column = lax.rem(y + shift, 4)
                outs[shift][pl.ds(0, 1), :] = spectra[4 * x + column]
                outs[shift][pl.ds(1, 1), :] = spectra[4 * partner + column]
                outs[shift][pl.ds(2, 6), :] = total[2:8]


def deal_kernel(*refs):
    pieces, outs, stack = refs[:4], refs[4:6], refs[6]
    y = here("y")
    for shift in range(4):
        stack[shift] = pieces[shift][...]
    for e in range(4):
        shift = lax.rem(y - e + 4, 4)
        for row in range(2):
            outs[row][pl.ds(e, 1), :] = stack[shift, pl.ds(row, 1), :]
            outs[row][pl.ds(4 + e, 1), :] = stack[shift, pl.ds(2, 1), :]


def vmem():
    return pl.BlockSpec(memory_space=pltpu.VMEM)


def smem():
    return pl.BlockSpec(memory_space=pltpu.SMEM)


def anywhere():
    return pl.BlockSpec(memory_space=pl.ANY)


def shape(*sizes):
    return jax.ShapeDtypeStruct(sizes, f32)


def params():
    return pltpu.CompilerParams(vmem_limit_bytes=VMEM_BYTES)


def cost(steps):
    return pl.CostEstimate(flops=int(steps * 1.4e9), bytes_accessed=int(steps * 2**20), transcendentals=0)


def prepare(pattern, onsite, coupling):
    return pl.pallas_call(
        prepare_kernel,
        out_shape=(shape(2, W, W), shape(W, W)),
        in_specs=[smem(), vmem(), vmem()],
        out_specs=[vmem(), vmem()],
        name="prepare",
    )(pattern, onsite, coupling)


def sweep(part, index, start, sets, bridge=None):
    first, stop = STEPS[part]
    count = stop - first
    arrays = list(sets)
    if bridge is not None:
        arrays.append(bridge)
    outs = [shape(count, W, W), shape(count, W, W), shape(count, 2, W, W)]
    outs.append(shape(2 * H2 + 8, W) if part > 1 else shape(2, W, W))
    return pl.pallas_call(
        functools.partial(sweep_kernel, part),
        out_shape=tuple(outs),
        in_specs=[smem(), vmem()] + [anywhere()] * len(arrays),
        out_specs=[anywhere(), anywhere(), anywhere(), vmem()],
        scratch_shapes=[
            pltpu.VMEM((count, W, W), f32),
            pltpu.VMEM((count, W, W), f32),
            pltpu.VMEM((count + 1, 2, W, W), f32),
            pltpu.SemaphoreType.DMA((count, 2)),
            pltpu.SemaphoreType.DMA((count, 3)),
        ],
        name="sweep_%d" % part,
        compiler_params=params(),
        cost_estimate=cost(count),
    )(index, start, *arrays)


def middle(index, arrived, wire_h, wire_m, store):
    return pl.pallas_call(
        middle_kernel,
        out_shape=(shape(2, W, W), shape(8, W), shape(1, W)),
        in_specs=[smem(), vmem(), anywhere(), anywhere(), anywhere()],
        out_specs=[vmem()] * 3,
        scratch_shapes=[
            pltpu.VMEM((W, W), f32),
            pltpu.VMEM((W, W), f32),
            pltpu.VMEM((2, W, W), f32),
            pltpu.SemaphoreType.DMA((3,)),
        ],
        name="middle",
        compiler_params=params(),
        cost_estimate=cost(2),
    )(index, arrived, wire_h, wire_m, store)


def outward(leg, index, start, earlier, totals, links, kept):
    first, stop = OUTWARD[leg]
    count = stop - first
    places = set()
    for t in range(first, stop):
        k = kept_at(15 - t)[0]
        places |= {(0, k), (2, k)}
        if t not in (7, 15):
            places.add((1, kept_at(14 - t)[0]))
    places = sorted(places)
    arrays = [*links, *(kept[k][kind] for kind, k in places)]
    outs = {
        0: [shape(2, W, W), shape(16, 1, W)],
        1: [shape(2 * H2 + 8, W), shape(16, 1, W)],
        2: [shape(8, W)] * 4,
    }[leg]
    return pl.pallas_call(
        functools.partial(outward_kernel, leg, places),
        out_shape=tuple(outs),
        in_specs=[smem()] + [vmem()] * (2 + len(totals)) + [anywhere()] * len(arrays),
        out_specs=[vmem()] * len(outs),
        scratch_shapes=[
            pltpu.VMEM((count, W, W), f32),
            pltpu.VMEM((count, W, W), f32),
            pltpu.VMEM((count, 2, W, W), f32),
            pltpu.VMEM((2, W, W), f32),
            pltpu.VMEM((16, 1, W), f32),
            pltpu.SemaphoreType.DMA((count, 3)),
        ],
        name="outward_%d" % leg,
        compiler_params=params(),
        cost_estimate=cost(1.2 * count),
    )(index, start, earlier, *totals, *arrays)


def deal(pieces):
    return pl.pallas_call(
        deal_kernel,
        out_shape=(shape(8, W), shape(8, W)),
        in_specs=[vmem()] * 4,
        out_specs=[vmem()] * 2,
        scratch_shapes=[pltpu.VMEM((4, 8, W), f32)],
        name="deal",
    )(*pieces)


AXES = ("half", "x", "y", "core")


def at(half, x, y, core):
    return ((half * 4 + x) * 4 + y) * 2 + core


def moved(value, move, chosen=lambda half, x, y, core: True):
    pairs = []
    for half in range(2):
        for x in range(4):
            for y in range(4):
                for core in range(2):
                    if chosen(half, x, y, core):
                        pairs.append((at(half, x, y, core), at(*move(half, x, y, core))))
    return lax.ppermute(value, AXES, pairs)


def is_task(half, x, y, core):
    return (x in (0, 3)) == (core == 0)


def outer_task(half, x, y, core):
    return is_task(half, x, y, core) and (x < 2) == (half == 0)


def inner_task(half, x, y, core):
    return is_task(half, x, y, core) and (x < 2) != (half == 0)


def along_y(value, shift, chosen=lambda *place: True):
    return moved(value, lambda half, x, y, core: (half, x, (y + shift) % 4, core), chosen)


def to_partner(value, chosen=lambda *place: True):
    return moved(value, lambda half, x, y, core: (half, x ^ 1, y, core), chosen)


def to_next(value, chosen):
    return moved(value, lambda half, x, y, core: (half, 3 - x, y, core), chosen)


def to_other_half(value, chosen):
    return moved(value, lambda half, x, y, core: (1 - half, 3 - x, y, core), chosen)


def across(value):
    return moved(value, lambda half, x, y, core: (half, x, y, 1 - core), lambda *place: not is_task(*place))


def after(value, other):
    return lax.optimization_barrier((value, other))[0]


def on_device(onsite, coupling, pattern, contact_rates, energy_index):
    x, y = here("x"), here("y")
    both, mine = prepare(pattern[0], onsite[0], coupling[0])
    near = to_partner(mine)
    left, right = along_y(mine, 1), along_y(mine, -1)
    opposite = jnp.concatenate([along_y(left[:H2], 1), along_y(right[H2:], -1)], axis=0)
    own_row = jnp.stack([right, opposite, left])
    near_row = jnp.stack([near, along_y(near, -1), to_partner(opposite), along_y(near, 1)])
    own_sent, near_sent = across(own_row), across(near_row)
    sets = (both, own_row, own_sent, near_row, near_sent)
    *first, carry = sweep(0, energy_index, contact_rates, sets)

    links = here("core") == 1
    own_links = jnp.concatenate([both[1:], jnp.where(links, own_row, own_sent)], axis=0)
    near_links = jnp.where(links, near_row, near_sent)
    row_links = jnp.where(lax.rem(x, 2) == 1, own_links, near_links)
    link = after(lax.dynamic_index_in_dim(row_links, lax.rem(7 - y, 4), 0, keepdims=False), carry)
    bridge = moved(
        link,
        lambda half, x, y, core: (half if x < 2 else 1, 3 - x, y, core),
        lambda half, x, y, core: is_task(half, x, y, core) and not (half == 1 and x >= 2),
    )
    *second, carry = sweep(1, energy_index, carry, sets)
    *edge, leaving = sweep(2, energy_index, carry, sets, bridge)
    arrived = to_next(leaving, outer_task)
    *inner, leaving = sweep(3, energy_index, arrived, sets, bridge)
    kept = [first, second, edge, inner]
    arrived = to_other_half(leaving, inner_task)
    carry, total, earlier = middle(energy_index, arrived, *inner)
    sent_total = to_other_half(
        total, lambda half, x, y, core: half == 1 and inner_task(half, x, y, core)
    )
    totals = [total, sent_total]
    carry, earlier = outward(0, energy_index, carry, earlier, [], [], kept)
    leaving, earlier = outward(1, energy_index, carry, earlier, totals, [bridge, link], kept)
    arrived = to_next(leaving, inner_task)
    pieces = outward(2, energy_index, arrived, earlier, totals, [], kept)

    pieces = [pieces[0]] + [along_y(pieces[shift], shift, is_task) for shift in (1, 2, 3)]
    own, other = deal(pieces)
    result = jnp.where(on_task(), own, to_partner(other, is_task))
    return result[:4][None], result[4:, 0]


def solution(mesh):
    fine = Mesh(mesh.devices.reshape(2, 4, 4, 2, 2), ("half", "x", "y", "plane", "core"))
    slab = ("half", "x", "y")
    part = ("plane", "core")
    return jax.shard_map(
        on_device,
        mesh=fine,
        in_specs=(P(slab), P(slab), P(slab), P(), P(part)),
        out_specs=(P(slab, part, None), P(part)),
        check_vma=False,
    )
```

```python
import functools
import jax
import jax.numpy as jnp
from jax import lax
from jax.experimental import pallas as pl
from jax.experimental.pallas import tpu as pltpu
from jax.sharding import Mesh
from jax.sharding import PartitionSpec as P

energy_floor = -0.2
energy_spacing = 0.0125
broadening = 0.3
W = 256
f32 = jnp.float32
b16 = jnp.bfloat16
VMEM_BYTES = 32 * 2**20


def dot_nt(left, right):
    return lax.dot_general(left, right, (((1,), (1,)), ((), ())), preferred_element_type=f32)


def dot_nn(left, right):
    return lax.dot_general(left, right, (((1,), (0,)), ((), ())), preferred_element_type=f32)


def split(value):
    high = value.astype(b16)
    return high, (value - high.astype(f32)).astype(b16)


def dot3(left, right, dot=dot_nt):
    return dot(left[0], right[0]) + (dot(left[1], right[0]) + dot(left[0], right[1]))


def cdot3(left, right, dot=dot_nt):
    (lr, li), (rr, ri) = left, right
    first = dot3(split(lr), split(rr), dot)
    second = dot3(split(li), split(ri), dot)
    summed = dot3(split(lr + li), split(rr + ri), dot)
    return first - second, summed - first - second


def eye_mask():
    rows = lax.broadcasted_iota(jnp.int32, (W, W), 0)
    columns = lax.broadcasted_iota(jnp.int32, (W, W), 1)
    return rows == columns


def diagonal_row(value):
    return jnp.sum(jnp.where(eye_mask(), value, 0.0), axis=0, keepdims=True)


def diagonal_and_rest(energy, onsite, sr, si):
    br = -(onsite + sr)
    bi = -si
    dr = energy + diagonal_row(br)
    di = broadening + diagonal_row(bi)
    scale = 1.0 / (dr * dr + di * di)
    dr, di = dr * scale, -di * scale
    mask = eye_mask()
    br = jnp.where(mask, 0.0, br)
    bi = jnp.where(mask, 0.0, bi)
    return br, bi, dr, di, br * dr - bi * di, br * di + bi * dr


def chain_step(energy, onsite, lead, sr, si):
    _, _, dr, di, fr, fi = diagonal_and_rest(energy, onsite, sr, si)
    frh, fih = fr.astype(b16), fi.astype(b16)
    leads = jnp.concatenate(split(lead), axis=0)
    pr, pi = dot_nt(leads, frh), dot_nt(leads, fih)
    pr, pi = pr[:W] + pr[W:], pi[:W] + pi[W:]
    prh, pih = pr.astype(b16), pi.astype(b16)
    qr = dot_nt(prh, frh) - dot_nt(pih, fih)
    qi = dot_nt(prh, fih) + dot_nt(pih, frh)
    x = lead - pr
    xr, xi = x * dr + pi * di, x * di - pi * dr
    return cdot3((xr, xi), (lead + qr, qi))


def spectral_row(energy, onsite, sr, si):
    br, bi, dr, di, fr, fi = diagonal_and_rest(energy, onsite, sr, si)
    frh, fih, brh, bih = (v.astype(b16) for v in (fr, fi, br, bi))
    yr = br - (dot_nt(frh, brh) - dot_nt(fih, bih))
    yi = bi - (dot_nt(frh, bih) + dot_nt(fih, brh))
    tr = jnp.sum(fr * yr - fi * yi, axis=1, keepdims=True)
    ti = jnp.sum(fr * yi + fi * yr, axis=1, keepdims=True)
    tr = diagonal_row(jnp.broadcast_to(tr, (W, W)))
    ti = diagonal_row(jnp.broadcast_to(ti, (W, W)))
    return -2.0 * (di + (dr * dr - di * di) * ti + 2.0 * dr * di * tr)


def crossing_row(energy, onsite, s0, s1, r0, r1):
    br, bi, dr, di, fr, fi = diagonal_and_rest(energy, onsite, s0 + r0, s1 + r1)
    f2r, f2i = cdot3((fr, fi), (fr, fi), dot_nn)
    f3r, f3i = cdot3((f2r, f2i), (fr, fi), dot_nn)
    one = jnp.where(eye_mask(), 1.0, 0.0)
    kr, ki = one - fr + f2r - f3r, -fi + f2i - f3i
    dcol_r = jnp.where(eye_mask(), dr, 0.0)
    dcol_i = jnp.where(eye_mask(), di, 0.0)
    dcol_r = jnp.sum(dcol_r, axis=1, keepdims=True)
    dcol_i = jnp.sum(dcol_i, axis=1, keepdims=True)
    gr, gi = dcol_r * kr - dcol_i * ki, dcol_r * ki + dcol_i * kr
    left, right = split(-2.0 * s1), split(-2.0 * r1)
    grs, gis = split(gr), split(gi)
    ar, ai = dot3(left, grs, dot_nn), dot3(left, gis, dot_nn)
    cr, ci = dot3(grs, right, dot_nt), dot3(gis, right, dot_nt)
    return jnp.sum(ar * cr + ai * ci, axis=0, keepdims=True)


H2 = W // 2


def here(name):
    if name == "x":
        return 2 * lax.axis_index("pair") + lax.axis_index("row")
    return lax.axis_index(name)


def on_task():
    x = here("x")
    return ((x == 0) | (x == 3)) == (here("core") == 0)


def is_outer():
    return (here("x") < 2) == (here("half") == 0)


def pack(sr, si, extra=0.0):
    rows = lax.broadcasted_iota(jnp.int32, (H2, H2), 0)
    columns = lax.broadcasted_iota(jnp.int32, (H2, H2), 1)

    def folded(value):
        low = value[H2:, H2:]
        fold = jnp.where(rows <= columns, value[:H2, :H2], low)
        diagonal = jnp.sum(jnp.where(rows == columns, low, 0.0), axis=0, keepdims=True)
        return jnp.concatenate([value[:H2, H2:], fold], axis=1), diagonal

    top, diagonal_top = folded(sr)
    bottom, diagonal_bottom = folded(si)
    row = jnp.broadcast_to(jnp.concatenate([diagonal_top, diagonal_bottom], axis=1), (8, W))
    last = jnp.where(lax.broadcasted_iota(jnp.int32, (8, W), 0) == 0, row, extra)
    return jnp.concatenate([top, bottom, last], axis=0)


def unpack(packed):
    rows = lax.broadcasted_iota(jnp.int32, (H2, H2), 0)
    columns = lax.broadcasted_iota(jnp.int32, (H2, H2), 1)

    def unfolded(value, diagonal):
        corner, fold = value[:, :H2], value[:, H2:]
        turned = fold.T
        first = jnp.where(rows <= columns, fold, turned)
        last = jnp.where(rows > columns, fold, jnp.where(rows < columns, turned, diagonal))
        top = jnp.concatenate([first, corner], axis=1)
        return jnp.concatenate([top, jnp.concatenate([corner.T, last], axis=1)], axis=0)

    return (
        unfolded(packed[:H2], packed[2 * H2 : 2 * H2 + 1, :H2]),
        unfolded(packed[H2 : 2 * H2], packed[2 * H2 : 2 * H2 + 1, H2:]),
    )


def prepare_kernel(pattern, onsite, coupling, both, mine):
    tiles = lax.broadcasted_iota(jnp.int32, (1, W), 1) // 64
    both[0] = onsite[...]
    for p in range(4):
        row = jnp.zeros((1, W), f32)
        for q in range(4):
            row = jnp.where(tiles == q, pattern[p, q].astype(f32), row)
        part = pl.ds(64 * p, 64)
        both[1, part, :] = coupling[part, :] * row
    mine[...] = both[here("core")]


def energy_of(index):
    return energy_floor + energy_spacing * index[here("y")].astype(f32)


STEPS = ((0, 3), (3, 7), (7, 8), (8, 16))
OUTWARD = ((1, 5), (5, 8), (8, 16))


def kept_at(t):
    part = next(k for k, (first, stop) in enumerate(STEPS) if first <= t < stop)
    return part, t - STEPS[part][0]


def sweep_kernel(part, *refs):
    first, stop = STEPS[part]
    count = stop - first
    refs = list(refs)
    index = refs.pop(0)
    start = refs.pop(0)
    both, own_mine, own_sent, near_mine, near_sent = (refs.pop(0) for _ in range(5))
    bridge = refs.pop(0) if part > 1 else None
    wire_h, wire_m, store, last = (refs.pop(0) for _ in range(4))
    link, link_sem = (refs.pop(0), refs.pop()) if part == 0 else (None, None)
    hbuf, mbuf, sbuf, in_sem, out_sem = refs
    half, y, core = here("half"), here("y"), here("core")
    energy = energy_of(index)

    def start_from(chunk, column, kind, target, sem):
        start_row(core == (0 if chunk in (0, 3) else 1), column, kind, target, sem)

    def start_row(own_row, column, kind, target, sem):
        away = lax.rem(column - y + 4, 4)

        @pl.when(own_row & (away == 0))
        def _():
            pltpu.make_async_copy(both.at[kind], target, sem).start()

        for here_too, own, near in ((core == kind, own_mine, near_mine), (core != kind, own_sent, near_sent)):

            @pl.when(own_row & (away != 0) & here_too)
            def _():
                pltpu.make_async_copy(own.at[jnp.maximum(away - 1, 0)], target, sem).start()

            @pl.when(~own_row & here_too)
            def _():
                pltpu.make_async_copy(near.at[away], target, sem).start()

    if part == 0:
        @pl.when(on_task())
        def _():
            start_row(lax.rem(here("x"), 2) == 1, 3, 1, link, link_sem.at[0])

    @pl.when(on_task() & (is_outer() if part < 3 else ~is_outer()))
    def _():
        for n in range(count):
            t = first + n
            start_from(t // 4, jnp.where(half == 0, t % 4, 3 - t % 4), 0, hbuf.at[n], in_sem.at[n, 0])
            if t % 4 < 3:
                start_from(t // 4, jnp.where(half == 0, t % 4, 2 - t % 4), 1, mbuf.at[n], in_sem.at[n, 1])
            else:

                @pl.when(half == 0)
                def _():
                    start_from(t // 4, 3, 1, mbuf.at[n], in_sem.at[n, 1])

                @pl.when(half != 0)
                def _():
                    if t % 8 == 7:
                        pltpu.make_async_copy(bridge, mbuf.at[n], in_sem.at[n, 1]).start()
                    else:
                        start_from(t // 4 + 1, 3, 1, mbuf.at[n], in_sem.at[n, 1])

        if part == 0:
            sbuf[0, 0] = jnp.zeros((W, W), f32)
            sbuf[0, 1] = jnp.where(eye_mask(), -0.5 * start[pl.ds(half, 1), :], 0.0)
        elif part < 3:
            sbuf[0] = start[...]
        else:
            sbuf[0, 0], sbuf[0, 1] = unpack(start[...])

        def kept(n):
            return (
                pltpu.make_async_copy(hbuf.at[n], wire_h.at[n], out_sem.at[n, 0]),
                pltpu.make_async_copy(mbuf.at[n], wire_m.at[n], out_sem.at[n, 1]),
                pltpu.make_async_copy(sbuf.at[n], store.at[n], out_sem.at[n, 2]),
            )

        def one(n, unused):
            pltpu.make_async_copy(wire_h.at[n], hbuf.at[n], in_sem.at[n, 0]).wait()
            pltpu.make_async_copy(wire_m.at[n], mbuf.at[n], in_sem.at[n, 1]).wait()
            for copy in kept(n):
                copy.start()
            m = mbuf[n]
            lead = jnp.where(half == 0, m.T, m)
            nr, ni = chain_step(energy, hbuf[n], lead, sbuf[n, 0], sbuf[n, 1])
            sbuf[n + 1, 0] = nr
            sbuf[n + 1, 1] = ni
            return 0

        lax.fori_loop(0, count, one, 0)
        if part > 1:
            last[...] = pack(sbuf[count, 0], sbuf[count, 1])
        else:
            last[...] = sbuf[count]
        for n in range(count):
            for copy in kept(n):
                copy.wait()

    if part == 0:

        @pl.when(on_task())
        def _():
            pltpu.make_async_copy(both.at[1], link, link_sem.at[0]).wait()


def middle_kernel(index, arrived, wire_h, wire_m, store, carried, crossing, spectrum, hbuf, mbuf, sbuf, in_sem):
    half = here("half")
    energy = energy_of(index)
    crossing[...] = jnp.zeros((8, W), f32)

    @pl.when(on_task() & ~is_outer())
    def _():
        copies = (
            pltpu.make_async_copy(wire_h.at[kept_at(15)[1]], hbuf, in_sem.at[0]),
            pltpu.make_async_copy(wire_m.at[kept_at(14)[1]], mbuf, in_sem.at[1]),
            pltpu.make_async_copy(store.at[kept_at(15)[1]], sbuf, in_sem.at[2]),
        )
        for copy in copies:
            copy.start()
        sr, si = unpack(arrived[...])
        for copy in copies:
            copy.wait()

        @pl.when(half != 0)
        def _():
            row = crossing_row(energy, hbuf[...], sr, si, sbuf[0], sbuf[1])
            crossing[...] = jnp.broadcast_to(jnp.sum(row, axis=1, keepdims=True), (8, W))

        spectrum[...] = spectral_row(energy, hbuf[...], sbuf[0] + sr, sbuf[1] + si)
        m = mbuf[...]
        lead = jnp.where(half == 0, m, m.T)
        nr, ni = chain_step(energy, hbuf[...], lead, sr, si)
        carried[0] = nr
        carried[1] = ni


def outward_kernel(leg, places, *refs):
    first, stop = OUTWARD[leg]
    count = stop - first
    refs = list(refs)
    index = refs.pop(0)
    start = refs.pop(0)
    earlier = refs.pop(0)
    totals = [refs.pop(0) for _ in range(2)] if leg else None
    links = [refs.pop(0) for _ in range(2)] if leg == 1 else None
    kept = {place: refs.pop(0) for place in places}
    outs = [refs.pop(0) for _ in range(1 if leg == 2 else 2)]
    hbuf, mbuf, sbuf, carried, spectra, in_sem = refs
    half = here("half")
    energy = energy_of(index)

    @pl.when(on_task() & (is_outer() if leg == 2 else ~is_outer()))
    def _():
        for n in range(count):
            t = first + n
            k, at_n = kept_at(15 - t)
            pltpu.make_async_copy(kept[0, k].at[at_n], hbuf.at[n], in_sem.at[n, 0]).start()
            pltpu.make_async_copy(kept[2, k].at[at_n], sbuf.at[n], in_sem.at[n, 2]).start()
            if t == 7:
                for side in range(2):

                    @pl.when(half == side)
                    def _():
                        pltpu.make_async_copy(links[side], mbuf.at[n], in_sem.at[n, 1]).start()

            elif t < 15:
                k, at_n = kept_at(14 - t)
                pltpu.make_async_copy(kept[1, k].at[at_n], mbuf.at[n], in_sem.at[n, 1]).start()
        if leg == 2:
            carried[0], carried[1] = unpack(start[...])
        else:
            carried[...] = start[...]
        if leg == 0:
            spectra[pl.ds(jnp.where(half == 0, 15, 0), 1)] = earlier[...][None]
        elif leg == 1:
            spectra[...] = earlier[...]

        def landed(n, link=True):
            pltpu.make_async_copy(hbuf.at[n], hbuf.at[n], in_sem.at[n, 0]).wait()
            pltpu.make_async_copy(sbuf.at[n], sbuf.at[n], in_sem.at[n, 2]).wait()
            if link:
                pltpu.make_async_copy(mbuf.at[n], mbuf.at[n], in_sem.at[n, 1]).wait()

        def spectrum(n):
            row = spectral_row(energy, hbuf[n], sbuf[n, 0] + carried[0], sbuf[n, 1] + carried[1])
            spectra[pl.ds(jnp.where(half == 0, 15 - first - n, first + n), 1)] = row[None]

        def one(n, unused):
            landed(n)
            spectrum(n)
            m = mbuf[n]
            lead = jnp.where(half == 0, m, m.T)
            nr, ni = chain_step(energy, hbuf[n], lead, carried[0], carried[1])
            carried[0] = nr
            carried[1] = ni
            return 0

        lax.fori_loop(0, count - (leg == 2), one, 0)
        if leg == 2:
            landed(count - 1, False)
            spectrum(count - 1)
        elif leg == 1:
            outs[0][...] = pack(carried[0], carried[1], totals[0][...] + totals[1][...])
            outs[1][...] = spectra[...]
        else:
            outs[0][...] = carried[...]
            outs[1][...] = spectra[...]

    if leg == 2:

        @pl.when(on_task())
        def _():
            @pl.when(~is_outer())
            def _():
                spectra[...] = earlier[...]

            outer_total = start[pl.ds(2 * H2, 8), :]
            total = jnp.where(is_outer(), outer_total, totals[0][...] + totals[1][...])
            base = 8 * lax.axis_index("pair")
            for place in range(8):
                outs[0][place, pl.ds(0, 1), :] = spectra[base + place]
                outs[0][place, pl.ds(1, 7), :] = total[1:8]


def deal_kernel(pieces, spectral, totals):
    row = jnp.where(lax.axis_index("pair") == 0, here("core"), 1 - here("core"))
    for e in range(4):
        spectral[pl.ds(e, 1), :] = pieces[4 * row + e, pl.ds(0, 1), :]
        totals[e] = jnp.max(pieces[4 * row + e, pl.ds(1, 1), :])


def vmem():
    return pl.BlockSpec(memory_space=pltpu.VMEM)


def smem():
    return pl.BlockSpec(memory_space=pltpu.SMEM)


def anywhere():
    return pl.BlockSpec(memory_space=pl.ANY)


def shape(*sizes):
    return jax.ShapeDtypeStruct(sizes, f32)


def params():
    return pltpu.CompilerParams(vmem_limit_bytes=VMEM_BYTES)


def cost(steps):
    return pl.CostEstimate(flops=int(steps * 1.4e9), bytes_accessed=int(steps * 2**20), transcendentals=0)


def prepare(pattern, onsite, coupling):
    return pl.pallas_call(
        prepare_kernel,
        out_shape=(shape(2, W, W), shape(W, W)),
        in_specs=[smem(), vmem(), vmem()],
        out_specs=[vmem(), vmem()],
        name="prepare",
    )(pattern, onsite, coupling)


def sweep(part, index, start, sets, bridge=None):
    first, stop = STEPS[part]
    count = stop - first
    arrays = list(sets)
    if bridge is not None:
        arrays.append(bridge)
    outs = [shape(count, W, W), shape(count, W, W), shape(count, 2, W, W)]
    outs.append(shape(2 * H2 + 8, W) if part > 1 else shape(2, W, W))
    specs = [anywhere(), anywhere(), anywhere(), vmem()]
    scratch = [
        pltpu.VMEM((count, W, W), f32),
        pltpu.VMEM((count, W, W), f32),
        pltpu.VMEM((count + 1, 2, W, W), f32),
        pltpu.SemaphoreType.DMA((count, 2)),
        pltpu.SemaphoreType.DMA((count, 3)),
    ]
    if part == 0:
        outs.append(shape(W, W))
        specs.append(anywhere())
        scratch.append(pltpu.SemaphoreType.DMA((1,)))
    return pl.pallas_call(
        functools.partial(sweep_kernel, part),
        out_shape=tuple(outs),
        in_specs=[smem(), vmem()] + [anywhere()] * len(arrays),
        out_specs=specs,
        scratch_shapes=scratch,
        name="sweep_%d" % part,
        compiler_params=params(),
        cost_estimate=cost(count),
    )(index, start, *arrays)


def middle(index, arrived, wire_h, wire_m, store):
    return pl.pallas_call(
        middle_kernel,
        out_shape=(shape(2, W, W), shape(8, W), shape(1, W)),
        in_specs=[smem(), vmem(), anywhere(), anywhere(), anywhere()],
        out_specs=[vmem()] * 3,
        scratch_shapes=[
            pltpu.VMEM((W, W), f32),
            pltpu.VMEM((W, W), f32),
            pltpu.VMEM((2, W, W), f32),
            pltpu.SemaphoreType.DMA((3,)),
        ],
        name="middle",
        compiler_params=params(),
        cost_estimate=cost(2),
    )(index, arrived, wire_h, wire_m, store)


def outward(leg, index, start, earlier, totals, links, kept):
    first, stop = OUTWARD[leg]
    count = stop - first
    places = set()
    for t in range(first, stop):
        k = kept_at(15 - t)[0]
        places |= {(0, k), (2, k)}
        if t not in (7, 15):
            places.add((1, kept_at(14 - t)[0]))
    places = sorted(places)
    arrays = [*links, *(kept[k][kind] for kind, k in places)]
    outs = {
        0: [shape(2, W, W), shape(16, 1, W)],
        1: [shape(2 * H2 + 8, W), shape(16, 1, W)],
        2: [shape(8, 8, W)],
    }[leg]
    return pl.pallas_call(
        functools.partial(outward_kernel, leg, places),
        out_shape=tuple(outs),
        in_specs=[smem()] + [vmem()] * (2 + len(totals)) + [anywhere()] * len(arrays),
        out_specs=[vmem()] * len(outs),
        scratch_shapes=[
            pltpu.VMEM((count, W, W), f32),
            pltpu.VMEM((count, W, W), f32),
            pltpu.VMEM((count, 2, W, W), f32),
            pltpu.VMEM((2, W, W), f32),
            pltpu.VMEM((16, 1, W), f32),
            pltpu.SemaphoreType.DMA((count, 3)),
        ],
        name="outward_%d" % leg,
        compiler_params=params(),
        cost_estimate=cost(1.2 * count),
    )(index, start, earlier, *totals, *arrays)


def deal(pieces):
    return pl.pallas_call(
        deal_kernel,
        out_shape=(shape(4, W), shape(4)),
        in_specs=[vmem()],
        out_specs=[vmem(), smem()],
        name="deal",
    )(pieces)


AXES = ("half", "pair", "row", "y", "core")


def at(half, x, y, core):
    return ((half * 4 + x) * 4 + y) * 2 + core


def moved(value, move, chosen=lambda half, x, y, core: True):
    pairs = []
    for half in range(2):
        for x in range(4):
            for y in range(4):
                for core in range(2):
                    if chosen(half, x, y, core):
                        pairs.append((at(half, x, y, core), at(*move(half, x, y, core))))
    return lax.ppermute(value, AXES, pairs)


def is_task(half, x, y, core):
    return (x in (0, 3)) == (core == 0)


def outer_task(half, x, y, core):
    return is_task(half, x, y, core) and (x < 2) == (half == 0)


def inner_task(half, x, y, core):
    return is_task(half, x, y, core) and (x < 2) != (half == 0)


def along_y(value, shift, chosen=lambda *place: True):
    return moved(value, lambda half, x, y, core: (half, x, (y + shift) % 4, core), chosen)


def to_partner(value, chosen=lambda *place: True):
    return moved(value, lambda half, x, y, core: (half, x ^ 1, y, core), chosen)


def to_next(value, chosen):
    return moved(value, lambda half, x, y, core: (half, 3 - x, y, core), chosen)


def to_other_half(value, chosen):
    return moved(value, lambda half, x, y, core: (1 - half, 3 - x, y, core), chosen)


def across(value):
    return moved(value, lambda half, x, y, core: (half, x, y, 1 - core), lambda *place: not is_task(*place))


def on_device(onsite, coupling, pattern, contact_rates, energy_index):
    both, mine = prepare(pattern[0], onsite[0], coupling[0])
    near = to_partner(mine)
    left, right = along_y(mine, 1), along_y(mine, -1)
    opposite = jnp.concatenate([along_y(left[:H2], 1), along_y(right[H2:], -1)], axis=0)
    own_row = jnp.stack([right, opposite, left])
    near_row = jnp.stack([near, along_y(near, -1), to_partner(opposite), along_y(near, 1)])
    own_sent, near_sent = across(own_row), across(near_row)
    sets = (both, own_row, own_sent, near_row, near_sent)
    *first, carry, link = sweep(0, energy_index, contact_rates, sets)
    bridge = moved(
        link,
        lambda half, x, y, core: (half if x < 2 else 1, 3 - x, y, core),
        lambda half, x, y, core: is_task(half, x, y, core) and not (half == 1 and x >= 2),
    )
    *second, carry = sweep(1, energy_index, carry, sets)
    *edge, leaving = sweep(2, energy_index, carry, sets, bridge)
    arrived = to_next(leaving, outer_task)
    *inner, leaving = sweep(3, energy_index, arrived, sets, bridge)
    kept = [first, second, edge, inner]
    arrived = to_other_half(leaving, inner_task)
    carry, total, earlier = middle(energy_index, arrived, *inner)
    sent_total = to_other_half(
        total, lambda half, x, y, core: half == 1 and inner_task(half, x, y, core)
    )
    totals = [total, sent_total]
    carry, earlier = outward(0, energy_index, carry, earlier, [], [], kept)
    leaving, earlier = outward(1, energy_index, carry, earlier, totals, [bridge, link], kept)
    arrived = to_next(leaving, inner_task)
    (pieces,) = outward(2, energy_index, arrived, earlier, totals, [], kept)
    pieces = lax.all_to_all(pieces, ("row", "y"), 0, 0)
    spectral, totals = deal(pieces)
    return spectral[None], totals


def solution(mesh):
    fine = Mesh(mesh.devices.reshape(2, 2, 2, 4, 2, 2), ("half", "pair", "row", "y", "plane", "core"))
    slab = ("half", "pair", "row", "y")
    part = ("plane", "core")
    return jax.shard_map(
        on_device,
        mesh=fine,
        in_specs=(P(slab), P(slab), P(slab), P(), P(part)),
        out_specs=(P(slab, part, None), P(part)),
        check_vma=False,
    )
```

```python
import functools
import jax
import jax.numpy as jnp
from jax import lax
from jax.experimental import pallas as pl
from jax.experimental.pallas import tpu as pltpu
from jax.sharding import Mesh
from jax.sharding import PartitionSpec as P

energy_floor = -0.2
energy_spacing = 0.0125
broadening = 0.3
W = 256
f32 = jnp.float32
b16 = jnp.bfloat16
VMEM_BYTES = 32 * 2**20


def dot_nt(left, right):
    return lax.dot_general(left, right, (((1,), (1,)), ((), ())), preferred_element_type=f32)


def dot_nn(left, right):
    return lax.dot_general(left, right, (((1,), (0,)), ((), ())), preferred_element_type=f32)


def split(value):
    high = value.astype(b16)
    return high, (value - high.astype(f32)).astype(b16)


def dot3(left, right, dot=dot_nt):
    return dot(left[0], right[0]) + (dot(left[1], right[0]) + dot(left[0], right[1]))


def cdot3(left, right, dot=dot_nt):
    (lr, li), (rr, ri) = left, right
    first = dot3(split(lr), split(rr), dot)
    second = dot3(split(li), split(ri), dot)
    summed = dot3(split(lr + li), split(rr + ri), dot)
    return first - second, summed - first - second


def eye_mask():
    rows = lax.broadcasted_iota(jnp.int32, (W, W), 0)
    columns = lax.broadcasted_iota(jnp.int32, (W, W), 1)
    return rows == columns


def diagonal_row(value):
    return jnp.sum(jnp.where(eye_mask(), value, 0.0), axis=0, keepdims=True)


def diagonal_and_rest(energy, onsite, sr, si):
    br = -(onsite + sr)
    bi = -si
    dr = energy + diagonal_row(br)
    di = broadening + diagonal_row(bi)
    scale = 1.0 / (dr * dr + di * di)
    dr, di = dr * scale, -di * scale
    mask = eye_mask()
    br = jnp.where(mask, 0.0, br)
    bi = jnp.where(mask, 0.0, bi)
    return br, bi, dr, di, br * dr - bi * di, br * di + bi * dr


def chain_step(energy, onsite, lead, sr, si):
    _, _, dr, di, fr, fi = diagonal_and_rest(energy, onsite, sr, si)
    frh, fih = fr.astype(b16), fi.astype(b16)
    leads = jnp.concatenate(split(lead), axis=0)
    pr, pi = dot_nt(leads, frh), dot_nt(leads, fih)
    pr, pi = pr[:W] + pr[W:], pi[:W] + pi[W:]
    prh, pih = pr.astype(b16), pi.astype(b16)
    qr = dot_nt(prh, frh) - dot_nt(pih, fih)
    qi = dot_nt(prh, fih) + dot_nt(pih, frh)
    x = lead - pr
    xr, xi = x * dr + pi * di, x * di - pi * dr
    return cdot3((xr, xi), (lead + qr, qi))


def spectral_row(energy, onsite, sr, si):
    br, bi, dr, di, fr, fi = diagonal_and_rest(energy, onsite, sr, si)
    frh, fih, brh, bih = (v.astype(b16) for v in (fr, fi, br, bi))
    yr = br - (dot_nt(frh, brh) - dot_nt(fih, bih))
    yi = bi - (dot_nt(frh, bih) + dot_nt(fih, brh))
    tr = jnp.sum(fr * yr - fi * yi, axis=1, keepdims=True)
    ti = jnp.sum(fr * yi + fi * yr, axis=1, keepdims=True)
    tr = diagonal_row(jnp.broadcast_to(tr, (W, W)))
    ti = diagonal_row(jnp.broadcast_to(ti, (W, W)))
    return -2.0 * (di + (dr * dr - di * di) * ti + 2.0 * dr * di * tr)


def crossing_row(energy, onsite, s0, s1, r0, r1):
    br, bi, dr, di, fr, fi = diagonal_and_rest(energy, onsite, s0 + r0, s1 + r1)
    f2r, f2i = cdot3((fr, fi), (fr, fi), dot_nn)
    f3r, f3i = cdot3((f2r, f2i), (fr, fi), dot_nn)
    one = jnp.where(eye_mask(), 1.0, 0.0)
    kr, ki = one - fr + f2r - f3r, -fi + f2i - f3i
    dcol_r = jnp.where(eye_mask(), dr, 0.0)
    dcol_i = jnp.where(eye_mask(), di, 0.0)
    dcol_r = jnp.sum(dcol_r, axis=1, keepdims=True)
    dcol_i = jnp.sum(dcol_i, axis=1, keepdims=True)
    gr, gi = dcol_r * kr - dcol_i * ki, dcol_r * ki + dcol_i * kr
    left, right = split(-2.0 * s1), split(-2.0 * r1)
    grs, gis = split(gr), split(gi)
    ar, ai = dot3(left, grs, dot_nn), dot3(left, gis, dot_nn)
    cr, ci = dot3(grs, right, dot_nt), dot3(gis, right, dot_nt)
    return jnp.sum(ar * cr + ai * ci, axis=0, keepdims=True)


H2 = W // 2


def here(name):
    if name == "x":
        return 2 * lax.axis_index("pair") + lax.axis_index("row")
    return lax.axis_index(name)


def on_task():
    x = here("x")
    return ((x == 0) | (x == 3)) == (here("core") == 0)


def is_outer():
    return (here("x") < 2) == (here("half") == 0)


def pack(sr, si, extra=0.0):
    rows = lax.broadcasted_iota(jnp.int32, (H2, H2), 0)
    columns = lax.broadcasted_iota(jnp.int32, (H2, H2), 1)

    def folded(value):
        low = value[H2:, H2:]
        fold = jnp.where(rows <= columns, value[:H2, :H2], low)
        diagonal = jnp.sum(jnp.where(rows == columns, low, 0.0), axis=0, keepdims=True)
        return jnp.concatenate([value[:H2, H2:], fold], axis=1), diagonal

    top, diagonal_top = folded(sr)
    bottom, diagonal_bottom = folded(si)
    row = jnp.broadcast_to(jnp.concatenate([diagonal_top, diagonal_bottom], axis=1), (8, W))
    last = jnp.where(lax.broadcasted_iota(jnp.int32, (8, W), 0) == 0, row, extra)
    return jnp.concatenate([top, bottom, last], axis=0)


def unpack(packed):
    rows = lax.broadcasted_iota(jnp.int32, (H2, H2), 0)
    columns = lax.broadcasted_iota(jnp.int32, (H2, H2), 1)

    def unfolded(value, diagonal):
        corner, fold = value[:, :H2], value[:, H2:]
        turned = fold.T
        first = jnp.where(rows <= columns, fold, turned)
        last = jnp.where(rows > columns, fold, jnp.where(rows < columns, turned, diagonal))
        top = jnp.concatenate([first, corner], axis=1)
        return jnp.concatenate([top, jnp.concatenate([corner.T, last], axis=1)], axis=0)

    return (
        unfolded(packed[:H2], packed[2 * H2 : 2 * H2 + 1, :H2]),
        unfolded(packed[H2 : 2 * H2], packed[2 * H2 : 2 * H2 + 1, H2:]),
    )


def prepare_kernel(pattern, onsite, coupling, both, mine):
    tiles = lax.broadcasted_iota(jnp.int32, (1, W), 1) // 64
    both[0] = onsite[...]
    for p in range(4):
        row = jnp.zeros((1, W), f32)
        for q in range(4):
            row = jnp.where(tiles == q, pattern[p, q].astype(f32), row)
        part = pl.ds(64 * p, 64)
        both[1, part, :] = coupling[part, :] * row
    mine[...] = both[here("core")]


def energy_of(index):
    return energy_floor + energy_spacing * index[here("y")].astype(f32)


STEPS = ((0, 2), (2, 7), (7, 8), (8, 16))
OUTWARD = ((1, 5), (5, 8), (8, 16))


def kept_at(t):
    part = next(k for k, (first, stop) in enumerate(STEPS) if first <= t < stop)
    return part, t - STEPS[part][0]


def sweep_kernel(part, *refs):
    first, stop = STEPS[part]
    count = stop - first
    refs = list(refs)
    index = refs.pop(0)
    start = refs.pop(0)
    both, own_onsite, own_links, near_mine, near_sent = (refs.pop(0) for _ in range(5))
    bridge = refs.pop(0) if part > 1 else None
    wire_h, wire_m, store, last = (refs.pop(0) for _ in range(4))
    link, link_sem = (refs.pop(0), refs.pop()) if part == 0 else (None, None)
    hbuf, mbuf, sbuf, in_sem, out_sem = refs
    half, y, core = here("half"), here("y"), here("core")
    energy = energy_of(index)

    def start_from(chunk, column, kind, target, sem):
        start_row(core == (0 if chunk in (0, 3) else 1), column, kind, target, sem)

    def start_row(own_row, column, kind, target, sem):
        away = lax.rem(column - y + 4, 4)

        @pl.when(own_row & (away == 0))
        def _():
            pltpu.make_async_copy(both.at[kind], target, sem).start()

        @pl.when(own_row & (away != 0))
        def _():
            source = (own_onsite, own_links)[kind].at[jnp.maximum(away - 1, 0)]
            pltpu.make_async_copy(source, target, sem).start()

        for here_too, near in ((core == kind, near_mine), (core != kind, near_sent)):

            @pl.when(~own_row & here_too)
            def _():
                pltpu.make_async_copy(near.at[away], target, sem).start()

    if part == 0:
        @pl.when(on_task())
        def _():
            start_row(lax.rem(here("x"), 2) == 1, 3, 1, link, link_sem.at[0])

    @pl.when(on_task() & (is_outer() if part < 3 else ~is_outer()))
    def _():
        for n in range(count):
            t = first + n
            start_from(t // 4, jnp.where(half == 0, t % 4, 3 - t % 4), 0, hbuf.at[n], in_sem.at[n, 0])
            if t % 4 < 3:
                start_from(t // 4, jnp.where(half == 0, t % 4, 2 - t % 4), 1, mbuf.at[n], in_sem.at[n, 1])
            else:

                @pl.when(half == 0)
                def _():
                    start_from(t // 4, 3, 1, mbuf.at[n], in_sem.at[n, 1])

                @pl.when(half != 0)
                def _():
                    if t % 8 == 7:
                        pltpu.make_async_copy(bridge, mbuf.at[n], in_sem.at[n, 1]).start()
                    else:
                        start_from(t // 4 + 1, 3, 1, mbuf.at[n], in_sem.at[n, 1])

        if part == 0:
            sbuf[0, 0] = jnp.zeros((W, W), f32)
            sbuf[0, 1] = jnp.where(eye_mask(), -0.5 * start[pl.ds(half, 1), :], 0.0)
        elif part < 3:
            sbuf[0] = start[...]
        else:
            sbuf[0, 0], sbuf[0, 1] = unpack(start[...])

        def kept(n):
            return (
                pltpu.make_async_copy(hbuf.at[n], wire_h.at[n], out_sem.at[n, 0]),
                pltpu.make_async_copy(mbuf.at[n], wire_m.at[n], out_sem.at[n, 1]),
                pltpu.make_async_copy(sbuf.at[n], store.at[n], out_sem.at[n, 2]),
            )

        def one(n, unused):
            pltpu.make_async_copy(wire_h.at[n], hbuf.at[n], in_sem.at[n, 0]).wait()
            pltpu.make_async_copy(wire_m.at[n], mbuf.at[n], in_sem.at[n, 1]).wait()
            for copy in kept(n):
                copy.start()
            m = mbuf[n]
            lead = jnp.where(half == 0, m.T, m)
            nr, ni = chain_step(energy, hbuf[n], lead, sbuf[n, 0], sbuf[n, 1])
            sbuf[n + 1, 0] = nr
            sbuf[n + 1, 1] = ni
            return 0

        lax.fori_loop(0, count, one, 0)
        if part > 1:
            last[...] = pack(sbuf[count, 0], sbuf[count, 1])
        else:
            last[...] = sbuf[count]
        for n in range(count):
            for copy in kept(n):
                copy.wait()

    if part == 0:

        @pl.when(on_task())
        def _():
            pltpu.make_async_copy(both.at[1], link, link_sem.at[0]).wait()


def middle_kernel(index, arrived, wire_h, wire_m, store, carried, crossing, spectrum, hbuf, mbuf, sbuf, in_sem):
    half = here("half")
    energy = energy_of(index)
    crossing[...] = jnp.zeros((8, W), f32)

    @pl.when(on_task() & ~is_outer())
    def _():
        copies = (
            pltpu.make_async_copy(wire_h.at[kept_at(15)[1]], hbuf, in_sem.at[0]),
            pltpu.make_async_copy(wire_m.at[kept_at(14)[1]], mbuf, in_sem.at[1]),
            pltpu.make_async_copy(store.at[kept_at(15)[1]], sbuf, in_sem.at[2]),
        )
        for copy in copies:
            copy.start()
        sr, si = unpack(arrived[...])
        for copy in copies:
            copy.wait()

        @pl.when(half != 0)
        def _():
            row = crossing_row(energy, hbuf[...], sr, si, sbuf[0], sbuf[1])
            crossing[...] = jnp.broadcast_to(jnp.sum(row, axis=1, keepdims=True), (8, W))

        spectrum[...] = spectral_row(energy, hbuf[...], sbuf[0] + sr, sbuf[1] + si)
        m = mbuf[...]
        lead = jnp.where(half == 0, m, m.T)
        nr, ni = chain_step(energy, hbuf[...], lead, sr, si)
        carried[0] = nr
        carried[1] = ni


def outward_kernel(leg, places, *refs):
    first, stop = OUTWARD[leg]
    count = stop - first
    refs = list(refs)
    index = refs.pop(0)
    start = refs.pop(0)
    earlier = refs.pop(0)
    totals = [refs.pop(0) for _ in range(2)] if leg else None
    links = [refs.pop(0) for _ in range(2)] if leg == 1 else None
    kept = {place: refs.pop(0) for place in places}
    outs = [refs.pop(0) for _ in range(1 if leg == 2 else 2)]
    hbuf, mbuf, sbuf, carried, spectra, in_sem = refs
    half = here("half")
    energy = energy_of(index)

    @pl.when(on_task() & (is_outer() if leg == 2 else ~is_outer()))
    def _():
        for n in range(count):
            t = first + n
            k, at_n = kept_at(15 - t)
            pltpu.make_async_copy(kept[0, k].at[at_n], hbuf.at[n], in_sem.at[n, 0]).start()
            pltpu.make_async_copy(kept[2, k].at[at_n], sbuf.at[n], in_sem.at[n, 2]).start()
            if t == 7:
                for side in range(2):

                    @pl.when(half == side)
                    def _():
                        pltpu.make_async_copy(links[side], mbuf.at[n], in_sem.at[n, 1]).start()

            elif t < 15:
                k, at_n = kept_at(14 - t)
                pltpu.make_async_copy(kept[1, k].at[at_n], mbuf.at[n], in_sem.at[n, 1]).start()
        if leg == 2:
            carried[0], carried[1] = unpack(start[...])
        else:
            carried[...] = start[...]
        if leg == 0:
            spectra[pl.ds(jnp.where(half == 0, 15, 0), 1)] = earlier[...][None]
        elif leg == 1:
            spectra[...] = earlier[...]

        def landed(n, link=True):
            pltpu.make_async_copy(hbuf.at[n], hbuf.at[n], in_sem.at[n, 0]).wait()
            pltpu.make_async_copy(sbuf.at[n], sbuf.at[n], in_sem.at[n, 2]).wait()
            if link:
                pltpu.make_async_copy(mbuf.at[n], mbuf.at[n], in_sem.at[n, 1]).wait()

        def spectrum(n):
            row = spectral_row(energy, hbuf[n], sbuf[n, 0] + carried[0], sbuf[n, 1] + carried[1])
            spectra[pl.ds(jnp.where(half == 0, 15 - first - n, first + n), 1)] = row[None]

        def one(n, unused):
            landed(n)
            spectrum(n)
            m = mbuf[n]
            lead = jnp.where(half == 0, m, m.T)
            nr, ni = chain_step(energy, hbuf[n], lead, carried[0], carried[1])
            carried[0] = nr
            carried[1] = ni
            return 0

        lax.fori_loop(0, count - (leg == 2), one, 0)
        if leg == 2:
            landed(count - 1, False)
            spectrum(count - 1)
        elif leg == 1:
            outs[0][...] = pack(carried[0], carried[1], totals[0][...] + totals[1][...])
            outs[1][...] = spectra[...]
        else:
            outs[0][...] = carried[...]
            outs[1][...] = spectra[...]

    if leg == 2:

        @pl.when(on_task())
        def _():
            @pl.when(~is_outer())
            def _():
                spectra[...] = earlier[...]

            outer_total = start[pl.ds(2 * H2, 8), :]
            total = jnp.where(is_outer(), outer_total, totals[0][...] + totals[1][...])
            base = 8 * lax.axis_index("pair")
            for place in range(8):
                outs[0][place, pl.ds(0, 1), :] = spectra[base + place]
                outs[0][place, pl.ds(1, 7), :] = total[1:8]


def deal_kernel(pieces, spectral, totals):
    row = jnp.where(lax.axis_index("pair") == 0, here("core"), 1 - here("core"))
    for e in range(4):
        spectral[pl.ds(e, 1), :] = pieces[4 * row + e, pl.ds(0, 1), :]
        totals[e] = jnp.max(pieces[4 * row + e, pl.ds(1, 1), :])


def vmem():
    return pl.BlockSpec(memory_space=pltpu.VMEM)


def smem():
    return pl.BlockSpec(memory_space=pltpu.SMEM)


def anywhere():
    return pl.BlockSpec(memory_space=pl.ANY)


def shape(*sizes):
    return jax.ShapeDtypeStruct(sizes, f32)


def params():
    return pltpu.CompilerParams(vmem_limit_bytes=VMEM_BYTES)


def cost(steps):
    return pl.CostEstimate(flops=int(steps * 1.4e9), bytes_accessed=int(steps * 2**20), transcendentals=0)


def prepare(pattern, onsite, coupling):
    return pl.pallas_call(
        prepare_kernel,
        out_shape=(shape(2, W, W), shape(W, W)),
        in_specs=[smem(), vmem(), vmem()],
        out_specs=[vmem(), vmem()],
        name="prepare",
    )(pattern, onsite, coupling)


def sweep(part, index, start, sets, bridge=None):
    first, stop = STEPS[part]
    count = stop - first
    arrays = list(sets)
    if bridge is not None:
        arrays.append(bridge)
    outs = [shape(count, W, W), shape(count, W, W), shape(count, 2, W, W)]
    outs.append(shape(2 * H2 + 8, W) if part > 1 else shape(2, W, W))
    specs = [anywhere(), anywhere(), anywhere(), vmem()]
    scratch = [
        pltpu.VMEM((count, W, W), f32),
        pltpu.VMEM((count, W, W), f32),
        pltpu.VMEM((count + 1, 2, W, W), f32),
        pltpu.SemaphoreType.DMA((count, 2)),
        pltpu.SemaphoreType.DMA((count, 3)),
    ]
    if part == 0:
        outs.append(shape(W, W))
        specs.append(anywhere())
        scratch.append(pltpu.SemaphoreType.DMA((1,)))
    return pl.pallas_call(
        functools.partial(sweep_kernel, part),
        out_shape=tuple(outs),
        in_specs=[smem(), vmem()] + [anywhere()] * len(arrays),
        out_specs=specs,
        scratch_shapes=scratch,
        name="sweep_%d" % part,
        compiler_params=params(),
        cost_estimate=cost(count),
    )(index, start, *arrays)


def middle(index, arrived, wire_h, wire_m, store):
    return pl.pallas_call(
        middle_kernel,
        out_shape=(shape(2, W, W), shape(8, W), shape(1, W)),
        in_specs=[smem(), vmem(), anywhere(), anywhere(), anywhere()],
        out_specs=[vmem()] * 3,
        scratch_shapes=[
            pltpu.VMEM((W, W), f32),
            pltpu.VMEM((W, W), f32),
            pltpu.VMEM((2, W, W), f32),
            pltpu.SemaphoreType.DMA((3,)),
        ],
        name="middle",
        compiler_params=params(),
        cost_estimate=cost(2),
    )(index, arrived, wire_h, wire_m, store)


def outward(leg, index, start, earlier, totals, links, kept):
    first, stop = OUTWARD[leg]
    count = stop - first
    places = set()
    for t in range(first, stop):
        k = kept_at(15 - t)[0]
        places |= {(0, k), (2, k)}
        if t not in (7, 15):
            places.add((1, kept_at(14 - t)[0]))
    places = sorted(places)
    arrays = [*links, *(kept[k][kind] for kind, k in places)]
    outs = {
        0: [shape(2, W, W), shape(16, 1, W)],
        1: [shape(2 * H2 + 8, W), shape(16, 1, W)],
        2: [shape(8, 8, W)],
    }[leg]
    return pl.pallas_call(
        functools.partial(outward_kernel, leg, places),
        out_shape=tuple(outs),
        in_specs=[smem()] + [vmem()] * (2 + len(totals)) + [anywhere()] * len(arrays),
        out_specs=[vmem()] * len(outs),
        scratch_shapes=[
            pltpu.VMEM((count, W, W), f32),
            pltpu.VMEM((count, W, W), f32),
            pltpu.VMEM((count, 2, W, W), f32),
            pltpu.VMEM((2, W, W), f32),
            pltpu.VMEM((16, 1, W), f32),
            pltpu.SemaphoreType.DMA((count, 3)),
        ],
        name="outward_%d" % leg,
        compiler_params=params(),
        cost_estimate=cost(1.2 * count),
    )(index, start, earlier, *totals, *arrays)


def deal(pieces):
    return pl.pallas_call(
        deal_kernel,
        out_shape=(shape(4, W), shape(4)),
        in_specs=[vmem()],
        out_specs=[vmem(), smem()],
        name="deal",
    )(pieces)


AXES = ("half", "pair", "row", "y", "core")


def at(half, x, y, core):
    return ((half * 4 + x) * 4 + y) * 2 + core


def moved(value, move, chosen=lambda half, x, y, core: True):
    pairs = []
    for half in range(2):
        for x in range(4):
            for y in range(4):
                for core in range(2):
                    if chosen(half, x, y, core):
                        pairs.append((at(half, x, y, core), at(*move(half, x, y, core))))
    return lax.ppermute(value, AXES, pairs)


def is_task(half, x, y, core):
    return (x in (0, 3)) == (core == 0)


def outer_task(half, x, y, core):
    return is_task(half, x, y, core) and (x < 2) == (half == 0)


def inner_task(half, x, y, core):
    return is_task(half, x, y, core) and (x < 2) != (half == 0)


def along_y(value, shift, chosen=lambda *place: True):
    return moved(value, lambda half, x, y, core: (half, x, (y + shift) % 4, core), chosen)


def to_partner(value, chosen=lambda *place: True):
    return moved(value, lambda half, x, y, core: (half, x ^ 1, y, core), chosen)


def to_next(value, chosen):
    return moved(value, lambda half, x, y, core: (half, 3 - x, y, core), chosen)


def to_other_half(value, chosen):
    return moved(value, lambda half, x, y, core: (1 - half, 3 - x, y, core), chosen)


def across(value):
    return moved(value, lambda half, x, y, core: (half, x, y, 1 - core), lambda *place: not is_task(*place))


def on_device(onsite, coupling, pattern, contact_rates, energy_index):
    both, mine = prepare(pattern[0], onsite[0], coupling[0])
    near = to_partner(mine)
    left, right = along_y(mine, 1), along_y(mine, -1)
    opposite = jnp.concatenate([along_y(left[:H2], 1), along_y(right[H2:], -1)], axis=0)
    own_row = jnp.stack([right, opposite, left])
    near_row = jnp.stack([near, along_y(near, -1), to_partner(opposite), along_y(near, 1)])
    own_sent, near_sent = across(own_row), across(near_row)
    brings_onsite = here("core") == 0
    own_onsite = jnp.where(brings_onsite, own_row, own_sent)
    own_links = jnp.where(brings_onsite, own_sent, own_row)
    sets = (both, own_onsite, own_links, near_row, near_sent)
    *first, carry, link = sweep(0, energy_index, contact_rates, sets)
    bridge = moved(
        link,
        lambda half, x, y, core: (half if x < 2 else 1, 3 - x, y, core),
        lambda half, x, y, core: is_task(half, x, y, core) and not (half == 1 and x >= 2),
    )
    *second, carry = sweep(1, energy_index, carry, sets)
    *edge, leaving = sweep(2, energy_index, carry, sets, bridge)
    arrived = to_next(leaving, outer_task)
    *inner, leaving = sweep(3, energy_index, arrived, sets, bridge)
    kept = [first, second, edge, inner]
    arrived = to_other_half(leaving, inner_task)
    carry, total, earlier = middle(energy_index, arrived, *inner)
    sent_total = to_other_half(
        total, lambda half, x, y, core: half == 1 and inner_task(half, x, y, core)
    )
    totals = [total, sent_total]
    carry, earlier = outward(0, energy_index, carry, earlier, [], [], kept)
    leaving, earlier = outward(1, energy_index, carry, earlier, totals, [bridge, link], kept)
    arrived = to_next(leaving, inner_task)
    (pieces,) = outward(2, energy_index, arrived, earlier, totals, [], kept)
    pieces = lax.all_to_all(pieces, ("row", "y"), 0, 0)
    spectral, totals = deal(pieces)
    return spectral[None], totals


def solution(mesh):
    fine = Mesh(mesh.devices.reshape(2, 2, 2, 4, 2, 2), ("half", "pair", "row", "y", "plane", "core"))
    slab = ("half", "pair", "row", "y")
    part = ("plane", "core")
    return jax.shard_map(
        on_device,
        mesh=fine,
        in_specs=(P(slab), P(slab), P(slab), P(), P(part)),
        out_specs=(P(slab, part, None), P(part)),
        check_vma=False,
    )
```

```python
import functools
import jax
import jax.numpy as jnp
from jax import lax
from jax.experimental import pallas as pl
from jax.experimental.pallas import tpu as pltpu
from jax.sharding import Mesh
from jax.sharding import PartitionSpec as P

energy_floor = -0.2
energy_spacing = 0.0125
broadening = 0.3
W = 256
f32 = jnp.float32
b16 = jnp.bfloat16
VMEM_BYTES = 32 * 2**20


def dot_nt(left, right):
    return lax.dot_general(left, right, (((1,), (1,)), ((), ())), preferred_element_type=f32)


def dot_nn(left, right):
    return lax.dot_general(left, right, (((1,), (0,)), ((), ())), preferred_element_type=f32)


def split(value):
    high = value.astype(b16)
    return high, (value - high.astype(f32)).astype(b16)


def dot3(left, right, dot=dot_nt):
    return dot(left[0], right[0]) + (dot(left[1], right[0]) + dot(left[0], right[1]))


def cdot3(left, right, dot=dot_nt):
    (lr, li), (rr, ri) = left, right
    first = dot3(split(lr), split(rr), dot)
    second = dot3(split(li), split(ri), dot)
    summed = dot3(split(lr + li), split(rr + ri), dot)
    return first - second, summed - first - second


def eye_mask():
    rows = lax.broadcasted_iota(jnp.int32, (W, W), 0)
    columns = lax.broadcasted_iota(jnp.int32, (W, W), 1)
    return rows == columns


def diagonal_row(value):
    return jnp.sum(jnp.where(eye_mask(), value, 0.0), axis=0, keepdims=True)


def diagonal_and_rest(energy, onsite, sr, si):
    br = -(onsite + sr)
    bi = -si
    dr = energy + diagonal_row(br)
    di = broadening + diagonal_row(bi)
    scale = 1.0 / (dr * dr + di * di)
    dr, di = dr * scale, -di * scale
    mask = eye_mask()
    br = jnp.where(mask, 0.0, br)
    bi = jnp.where(mask, 0.0, bi)
    return br, bi, dr, di, br * dr - bi * di, br * di + bi * dr


def chain_step(energy, onsite, lead, sr, si):
    _, _, dr, di, fr, fi = diagonal_and_rest(energy, onsite, sr, si)
    frh, fih = fr.astype(b16), fi.astype(b16)
    leads = jnp.concatenate(split(lead), axis=0)
    pr, pi = dot_nt(leads, frh), dot_nt(leads, fih)
    pr, pi = pr[:W] + pr[W:], pi[:W] + pi[W:]
    prh, pih = pr.astype(b16), pi.astype(b16)
    qr = dot_nt(prh, frh) - dot_nt(pih, fih)
    qi = dot_nt(prh, fih) + dot_nt(pih, frh)
    x = lead - pr
    xr, xi = x * dr + pi * di, x * di - pi * dr
    return cdot3((xr, xi), (lead + qr, qi))


def spectral_row(energy, onsite, sr, si):
    br, bi, dr, di, fr, fi = diagonal_and_rest(energy, onsite, sr, si)
    frh, fih, brh, bih = (v.astype(b16) for v in (fr, fi, br, bi))
    yr = br - (dot_nt(frh, brh) - dot_nt(fih, bih))
    yi = bi - (dot_nt(frh, bih) + dot_nt(fih, brh))
    tr = jnp.sum(fr * yr - fi * yi, axis=1, keepdims=True)
    ti = jnp.sum(fr * yi + fi * yr, axis=1, keepdims=True)
    tr = diagonal_row(jnp.broadcast_to(tr, (W, W)))
    ti = diagonal_row(jnp.broadcast_to(ti, (W, W)))
    return -2.0 * (di + (dr * dr - di * di) * ti + 2.0 * dr * di * tr)


def crossing_row(energy, onsite, s0, s1, r0, r1):
    br, bi, dr, di, fr, fi = diagonal_and_rest(energy, onsite, s0 + r0, s1 + r1)
    f2r, f2i = cdot3((fr, fi), (fr, fi), dot_nn)
    f3r, f3i = cdot3((f2r, f2i), (fr, fi), dot_nn)
    one = jnp.where(eye_mask(), 1.0, 0.0)
    kr, ki = one - fr + f2r - f3r, -fi + f2i - f3i
    dcol_r = jnp.where(eye_mask(), dr, 0.0)
    dcol_i = jnp.where(eye_mask(), di, 0.0)
    dcol_r = jnp.sum(dcol_r, axis=1, keepdims=True)
    dcol_i = jnp.sum(dcol_i, axis=1, keepdims=True)
    gr, gi = dcol_r * kr - dcol_i * ki, dcol_r * ki + dcol_i * kr
    left, right = split(-2.0 * s1), split(-2.0 * r1)
    grs, gis = split(gr), split(gi)
    ar, ai = dot3(left, grs, dot_nn), dot3(left, gis, dot_nn)
    cr, ci = dot3(grs, right, dot_nt), dot3(gis, right, dot_nt)
    return jnp.sum(ar * cr + ai * ci, axis=0, keepdims=True)


H2 = W // 2


def here(name):
    if name == "x":
        return 2 * lax.axis_index("pair") + lax.axis_index("row")
    return lax.axis_index(name)


def on_task():
    x = here("x")
    return ((x == 0) | (x == 3)) == (here("core") == 0)


def is_outer():
    return (here("x") < 2) == (here("half") == 0)


def pack(sr, si, extra=0.0):
    rows = lax.broadcasted_iota(jnp.int32, (H2, H2), 0)
    columns = lax.broadcasted_iota(jnp.int32, (H2, H2), 1)

    def folded(value):
        low = value[H2:, H2:]
        fold = jnp.where(rows <= columns, value[:H2, :H2], low)
        diagonal = jnp.sum(jnp.where(rows == columns, low, 0.0), axis=0, keepdims=True)
        return jnp.concatenate([value[:H2, H2:], fold], axis=1), diagonal

    top, diagonal_top = folded(sr)
    bottom, diagonal_bottom = folded(si)
    row = jnp.broadcast_to(jnp.concatenate([diagonal_top, diagonal_bottom], axis=1), (8, W))
    last = jnp.where(lax.broadcasted_iota(jnp.int32, (8, W), 0) == 0, row, extra)
    return jnp.concatenate([top, bottom, last], axis=0)


def unpack(packed):
    rows = lax.broadcasted_iota(jnp.int32, (H2, H2), 0)
    columns = lax.broadcasted_iota(jnp.int32, (H2, H2), 1)

    def unfolded(value, diagonal):
        corner, fold = value[:, :H2], value[:, H2:]
        turned = fold.T
        first = jnp.where(rows <= columns, fold, turned)
        last = jnp.where(rows > columns, fold, jnp.where(rows < columns, turned, diagonal))
        top = jnp.concatenate([first, corner], axis=1)
        return jnp.concatenate([top, jnp.concatenate([corner.T, last], axis=1)], axis=0)

    return (
        unfolded(packed[:H2], packed[2 * H2 : 2 * H2 + 1, :H2]),
        unfolded(packed[H2 : 2 * H2], packed[2 * H2 : 2 * H2 + 1, H2:]),
    )


def prepare_kernel(pattern, onsite, coupling, both, mine):
    tiles = lax.broadcasted_iota(jnp.int32, (1, W), 1) // 64
    both[0] = onsite[...]
    for p in range(4):
        row = jnp.zeros((1, W), f32)
        for q in range(4):
            row = jnp.where(tiles == q, pattern[p, q].astype(f32), row)
        part = pl.ds(64 * p, 64)
        both[1, part, :] = coupling[part, :] * row
    mine[...] = both[here("core")]


def energy_of(index):
    return energy_floor + energy_spacing * index[here("y")].astype(f32)


STEPS = ((0, 7), (7, 8), (8, 16))
OUTWARD = ((1, 5), (5, 8), (8, 16))


def kept_at(t):
    part = next(k for k, (first, stop) in enumerate(STEPS) if first <= t < stop)
    return part, t - STEPS[part][0]


def sweep_kernel(part, *refs):
    first, stop = STEPS[part]
    count = stop - first
    refs = list(refs)
    index = refs.pop(0)
    start = refs.pop(0)
    both, own_onsite, own_links, near_mine, near_sent = (refs.pop(0) for _ in range(5))
    bridge = refs.pop(0) if part else None
    wire_h, wire_m, store, last = (refs.pop(0) for _ in range(4))
    hbuf, mbuf, sbuf, in_sem, out_sem = refs
    half, y, core = here("half"), here("y"), here("core")
    energy = energy_of(index)

    def start_from(chunk, column, kind, target, sem):
        away = lax.rem(column - y + 4, 4)
        own_row = core == (0 if chunk in (0, 3) else 1)

        @pl.when(own_row & (away == 0))
        def _():
            pltpu.make_async_copy(both.at[kind], target, sem).start()

        @pl.when(own_row & (away != 0))
        def _():
            source = (own_onsite, own_links)[kind].at[jnp.maximum(away - 1, 0)]
            pltpu.make_async_copy(source, target, sem).start()

        for here_too, near in ((core == kind, near_mine), (core != kind, near_sent)):

            @pl.when(~own_row & here_too)
            def _():
                pltpu.make_async_copy(near.at[away], target, sem).start()

    @pl.when(on_task() & (is_outer() if part < 2 else ~is_outer()))
    def _():
        for n in range(count):
            t = first + n
            start_from(t // 4, jnp.where(half == 0, t % 4, 3 - t % 4), 0, hbuf.at[n], in_sem.at[n, 0])
            if t % 4 < 3:
                start_from(t // 4, jnp.where(half == 0, t % 4, 2 - t % 4), 1, mbuf.at[n], in_sem.at[n, 1])
            else:

                @pl.when(half == 0)
                def _():
                    start_from(t // 4, 3, 1, mbuf.at[n], in_sem.at[n, 1])

                @pl.when(half != 0)
                def _():
                    if t % 8 == 7:
                        pltpu.make_async_copy(bridge, mbuf.at[n], in_sem.at[n, 1]).start()
                    else:
                        start_from(t // 4 + 1, 3, 1, mbuf.at[n], in_sem.at[n, 1])

        if part == 0:
            sbuf[0, 0] = jnp.zeros((W, W), f32)
            sbuf[0, 1] = jnp.where(eye_mask(), -0.5 * start[pl.ds(half, 1), :], 0.0)
        elif part == 1:
            sbuf[0] = start[...]
        else:
            sbuf[0, 0], sbuf[0, 1] = unpack(start[...])

        def kept(n):
            return (
                pltpu.make_async_copy(hbuf.at[n], wire_h.at[n], out_sem.at[n, 0]),
                pltpu.make_async_copy(mbuf.at[n], wire_m.at[n], out_sem.at[n, 1]),
                pltpu.make_async_copy(sbuf.at[n], store.at[n], out_sem.at[n, 2]),
            )

        def one(n, unused):
            pltpu.make_async_copy(wire_h.at[n], hbuf.at[n], in_sem.at[n, 0]).wait()
            pltpu.make_async_copy(wire_m.at[n], mbuf.at[n], in_sem.at[n, 1]).wait()
            for copy in kept(n):
                copy.start()
            m = mbuf[n]
            lead = jnp.where(half == 0, m.T, m)
            nr, ni = chain_step(energy, hbuf[n], lead, sbuf[n, 0], sbuf[n, 1])
            sbuf[n + 1, 0] = nr
            sbuf[n + 1, 1] = ni
            return 0

        lax.fori_loop(0, count, one, 0)
        if part:
            last[...] = pack(sbuf[count, 0], sbuf[count, 1])
        else:
            last[...] = sbuf[count]
        for n in range(count):
            for copy in kept(n):
                copy.wait()


def middle_kernel(index, arrived, wire_h, wire_m, store, carried, crossing, spectrum, hbuf, mbuf, sbuf, in_sem):
    half = here("half")
    energy = energy_of(index)
    crossing[...] = jnp.zeros((8, W), f32)

    @pl.when(on_task() & ~is_outer())
    def _():
        copies = (
            pltpu.make_async_copy(wire_h.at[kept_at(15)[1]], hbuf, in_sem.at[0]),
            pltpu.make_async_copy(wire_m.at[kept_at(14)[1]], mbuf, in_sem.at[1]),
            pltpu.make_async_copy(store.at[kept_at(15)[1]], sbuf, in_sem.at[2]),
        )
        for copy in copies:
            copy.start()
        sr, si = unpack(arrived[...])
        for copy in copies:
            copy.wait()

        @pl.when(half != 0)
        def _():
            row = crossing_row(energy, hbuf[...], sr, si, sbuf[0], sbuf[1])
            crossing[...] = jnp.broadcast_to(jnp.sum(row, axis=1, keepdims=True), (8, W))

        spectrum[...] = spectral_row(energy, hbuf[...], sbuf[0] + sr, sbuf[1] + si)
        m = mbuf[...]
        lead = jnp.where(half == 0, m, m.T)
        nr, ni = chain_step(energy, hbuf[...], lead, sr, si)
        carried[0] = nr
        carried[1] = ni


def outward_kernel(leg, places, *refs):
    first, stop = OUTWARD[leg]
    count = stop - first
    refs = list(refs)
    index = refs.pop(0)
    start = refs.pop(0)
    earlier = refs.pop(0)
    totals = [refs.pop(0) for _ in range(2)] if leg else None
    links = [refs.pop(0) for _ in range(3)] if leg == 1 else None
    kept = {place: refs.pop(0) for place in places}
    outs = [refs.pop(0) for _ in range(1 if leg == 2 else 2)]
    hbuf, mbuf, sbuf, carried, spectra, in_sem = refs
    half = here("half")
    energy = energy_of(index)

    @pl.when(on_task() & (is_outer() if leg == 2 else ~is_outer()))
    def _():
        for n in range(count):
            t = first + n
            k, at_n = kept_at(15 - t)
            pltpu.make_async_copy(kept[0, k].at[at_n], hbuf.at[n], in_sem.at[n, 0]).start()
            pltpu.make_async_copy(kept[2, k].at[at_n], sbuf.at[n], in_sem.at[n, 2]).start()
            if t == 7:
                away = lax.rem(7 - here("y"), 4)
                upper, brings = half != 0, here("core") != 0
                for wanted, source in (
                    (~upper, links[0]),
                    (upper & brings, links[1]),
                    (upper & ~brings, links[2].at[away]),
                ):

                    @pl.when(wanted)
                    def _():
                        pltpu.make_async_copy(source, mbuf.at[n], in_sem.at[n, 1]).start()

            elif t < 15:
                k, at_n = kept_at(14 - t)
                pltpu.make_async_copy(kept[1, k].at[at_n], mbuf.at[n], in_sem.at[n, 1]).start()
        if leg == 2:
            carried[0], carried[1] = unpack(start[...])
        else:
            carried[...] = start[...]
        if leg == 0:
            spectra[pl.ds(jnp.where(half == 0, 15, 0), 1)] = earlier[...][None]
        elif leg == 1:
            spectra[...] = earlier[...]

        def landed(n, link=True):
            pltpu.make_async_copy(hbuf.at[n], hbuf.at[n], in_sem.at[n, 0]).wait()
            pltpu.make_async_copy(sbuf.at[n], sbuf.at[n], in_sem.at[n, 2]).wait()
            if link:
                pltpu.make_async_copy(mbuf.at[n], mbuf.at[n], in_sem.at[n, 1]).wait()

        def spectrum(n):
            row = spectral_row(energy, hbuf[n], sbuf[n, 0] + carried[0], sbuf[n, 1] + carried[1])
            spectra[pl.ds(jnp.where(half == 0, 15 - first - n, first + n), 1)] = row[None]

        def one(n, unused):
            landed(n)
            spectrum(n)
            m = mbuf[n]
            lead = jnp.where(half == 0, m, m.T)
            nr, ni = chain_step(energy, hbuf[n], lead, carried[0], carried[1])
            carried[0] = nr
            carried[1] = ni
            return 0

        lax.fori_loop(0, count - (leg == 2), one, 0)
        if leg == 2:
            landed(count - 1, False)
            spectrum(count - 1)
        elif leg == 1:
            outs[0][...] = pack(carried[0], carried[1], totals[0][...] + totals[1][...])
            outs[1][...] = spectra[...]
        else:
            outs[0][...] = carried[...]
            outs[1][...] = spectra[...]

    if leg == 2:

        @pl.when(on_task())
        def _():
            @pl.when(~is_outer())
            def _():
                spectra[...] = earlier[...]

            outer_total = start[pl.ds(2 * H2, 8), :]
            total = jnp.where(is_outer(), outer_total, totals[0][...] + totals[1][...])
            base = 8 * lax.axis_index("pair")
            for place in range(8):
                outs[0][place, pl.ds(0, 1), :] = spectra[base + place]
                outs[0][place, pl.ds(1, 7), :] = total[1:8]


def deal_kernel(pieces, spectral, totals):
    row = jnp.where(lax.axis_index("pair") == 0, here("core"), 1 - here("core"))
    for e in range(4):
        spectral[pl.ds(e, 1), :] = pieces[4 * row + e, pl.ds(0, 1), :]
        totals[e] = jnp.max(pieces[4 * row + e, pl.ds(1, 1), :])


def vmem():
    return pl.BlockSpec(memory_space=pltpu.VMEM)


def smem():
    return pl.BlockSpec(memory_space=pltpu.SMEM)


def anywhere():
    return pl.BlockSpec(memory_space=pl.ANY)


def shape(*sizes):
    return jax.ShapeDtypeStruct(sizes, f32)


def params():
    return pltpu.CompilerParams(vmem_limit_bytes=VMEM_BYTES)


def cost(steps):
    return pl.CostEstimate(flops=int(steps * 1.4e9), bytes_accessed=int(steps * 2**20), transcendentals=0)


def prepare(pattern, onsite, coupling):
    return pl.pallas_call(
        prepare_kernel,
        out_shape=(shape(2, W, W), shape(W, W)),
        in_specs=[smem(), vmem(), vmem()],
        out_specs=[vmem(), vmem()],
        name="prepare",
    )(pattern, onsite, coupling)


def sweep(part, index, start, sets, bridge=None):
    first, stop = STEPS[part]
    count = stop - first
    arrays = list(sets)
    if bridge is not None:
        arrays.append(bridge)
    outs = [shape(count, W, W), shape(count, W, W), shape(count, 2, W, W)]
    outs.append(shape(2 * H2 + 8, W) if part else shape(2, W, W))
    specs = [anywhere(), anywhere(), anywhere(), vmem()]
    scratch = [
        pltpu.VMEM((count, W, W), f32),
        pltpu.VMEM((count, W, W), f32),
        pltpu.VMEM((count + 1, 2, W, W), f32),
        pltpu.SemaphoreType.DMA((count, 2)),
        pltpu.SemaphoreType.DMA((count, 3)),
    ]
    return pl.pallas_call(
        functools.partial(sweep_kernel, part),
        out_shape=tuple(outs),
        in_specs=[smem(), vmem()] + [anywhere()] * len(arrays),
        out_specs=specs,
        scratch_shapes=scratch,
        name="sweep_%d" % part,
        compiler_params=params(),
        cost_estimate=cost(count),
    )(index, start, *arrays)


def middle(index, arrived, wire_h, wire_m, store):
    return pl.pallas_call(
        middle_kernel,
        out_shape=(shape(2, W, W), shape(8, W), shape(1, W)),
        in_specs=[smem(), vmem(), anywhere(), anywhere(), anywhere()],
        out_specs=[vmem()] * 3,
        scratch_shapes=[
            pltpu.VMEM((W, W), f32),
            pltpu.VMEM((W, W), f32),
            pltpu.VMEM((2, W, W), f32),
            pltpu.SemaphoreType.DMA((3,)),
        ],
        name="middle",
        compiler_params=params(),
        cost_estimate=cost(2),
    )(index, arrived, wire_h, wire_m, store)


def outward(leg, index, start, earlier, totals, links, kept):
    first, stop = OUTWARD[leg]
    count = stop - first
    places = set()
    for t in range(first, stop):
        k = kept_at(15 - t)[0]
        places |= {(0, k), (2, k)}
        if t not in (7, 15):
            places.add((1, kept_at(14 - t)[0]))
    places = sorted(places)
    arrays = [*links, *(kept[k][kind] for kind, k in places)]
    outs = {
        0: [shape(2, W, W), shape(16, 1, W)],
        1: [shape(2 * H2 + 8, W), shape(16, 1, W)],
        2: [shape(8, 8, W)],
    }[leg]
    return pl.pallas_call(
        functools.partial(outward_kernel, leg, places),
        out_shape=tuple(outs),
        in_specs=[smem()] + [vmem()] * (2 + len(totals)) + [anywhere()] * len(arrays),
        out_specs=[vmem()] * len(outs),
        scratch_shapes=[
            pltpu.VMEM((count, W, W), f32),
            pltpu.VMEM((count, W, W), f32),
            pltpu.VMEM((count, 2, W, W), f32),
            pltpu.VMEM((2, W, W), f32),
            pltpu.VMEM((16, 1, W), f32),
            pltpu.SemaphoreType.DMA((count, 3)),
        ],
        name="outward_%d" % leg,
        compiler_params=params(),
        cost_estimate=cost(1.2 * count),
    )(index, start, earlier, *totals, *arrays)


def deal(pieces):
    return pl.pallas_call(
        deal_kernel,
        out_shape=(shape(4, W), shape(4)),
        in_specs=[vmem()],
        out_specs=[vmem(), smem()],
        name="deal",
    )(pieces)


AXES = ("half", "pair", "row", "y", "core")


def at(half, x, y, core):
    return ((half * 4 + x) * 4 + y) * 2 + core


def moved(value, move, chosen=lambda half, x, y, core: True):
    pairs = []
    for half in range(2):
        for x in range(4):
            for y in range(4):
                for core in range(2):
                    if chosen(half, x, y, core):
                        pairs.append((at(half, x, y, core), at(*move(half, x, y, core))))
    return lax.ppermute(value, AXES, pairs)


def is_task(half, x, y, core):
    return (x in (0, 3)) == (core == 0)


def outer_task(half, x, y, core):
    return is_task(half, x, y, core) and (x < 2) == (half == 0)


def inner_task(half, x, y, core):
    return is_task(half, x, y, core) and (x < 2) != (half == 0)


def along_y(value, shift, chosen=lambda *place: True):
    return moved(value, lambda half, x, y, core: (half, x, (y + shift) % 4, core), chosen)


def to_partner(value, chosen=lambda *place: True):
    return moved(value, lambda half, x, y, core: (half, x ^ 1, y, core), chosen)


def to_next(value, chosen):
    return moved(value, lambda half, x, y, core: (half, 3 - x, y, core), chosen)


def to_other_half(value, chosen):
    return moved(value, lambda half, x, y, core: (1 - half, 3 - x, y, core), chosen)


def across(value):
    return moved(value, lambda half, x, y, core: (half, x, y, 1 - core), lambda *place: not is_task(*place))


def on_device(onsite, coupling, pattern, contact_rates, energy_index):
    both, mine = prepare(pattern[0], onsite[0], coupling[0])
    near = to_partner(mine)
    left, right = along_y(mine, 1), along_y(mine, -1)
    opposite = jnp.concatenate([along_y(left[:H2], 1), along_y(right[H2:], -1)], axis=0)
    own_row = jnp.stack([right, opposite, left])
    near_row = jnp.stack([near, along_y(near, -1), to_partner(opposite), along_y(near, 1)])
    own_sent, near_sent = across(own_row), across(near_row)
    brings_onsite = here("core") == 0
    own_onsite = jnp.where(brings_onsite, own_row, own_sent)
    own_links = jnp.where(brings_onsite, own_sent, own_row)
    sets = (both, own_onsite, own_links, near_row, near_sent)
    x, y = here("x"), here("y")
    row_links = jnp.where(lax.rem(x, 2) == 1, jnp.concatenate([mine[None], own_row], axis=0), near_row)
    link = lax.dynamic_index_in_dim(row_links, lax.rem(7 - y, 4), 0, keepdims=False)
    bridge = moved(
        link,
        lambda half, x, y, core: (half if x < 2 else 1, 3 - x, y, 0 if x in (0, 3) else 1),
        lambda half, x, y, core: core == 1 and not (half == 1 and x >= 2),
    )
    *first, carry = sweep(0, energy_index, contact_rates, sets)
    *edge, leaving = sweep(1, energy_index, carry, sets, bridge)
    arrived = to_next(leaving, outer_task)
    *inner, leaving = sweep(2, energy_index, arrived, sets, bridge)
    kept = [first, edge, inner]
    arrived = to_other_half(leaving, inner_task)
    carry, total, earlier = middle(energy_index, arrived, *inner)
    sent_total = to_other_half(
        total, lambda half, x, y, core: half == 1 and inner_task(half, x, y, core)
    )
    totals = [total, sent_total]
    carry, earlier = outward(0, energy_index, carry, earlier, [], [], kept)
    leaving, earlier = outward(1, energy_index, carry, earlier, totals, [bridge, link, near_sent], kept)
    arrived = to_next(leaving, inner_task)
    (pieces,) = outward(2, energy_index, arrived, earlier, totals, [], kept)
    pieces = lax.all_to_all(pieces, ("row", "y"), 0, 0)
    spectral, totals = deal(pieces)
    return spectral[None], totals


def solution(mesh):
    fine = Mesh(mesh.devices.reshape(2, 2, 2, 4, 2, 2), ("half", "pair", "row", "y", "plane", "core"))
    slab = ("half", "pair", "row", "y")
    part = ("plane", "core")
    return jax.shard_map(
        on_device,
        mesh=fine,
        in_specs=(P(slab), P(slab), P(slab), P(), P(part)),
        out_specs=(P(slab, part, None), P(part)),
        check_vma=False,
    )
```

```python
import functools
import jax
import jax.numpy as jnp
from jax import lax
from jax.experimental import pallas as pl
from jax.experimental.pallas import tpu as pltpu
from jax.sharding import Mesh
from jax.sharding import PartitionSpec as P

energy_floor = -0.2
energy_spacing = 0.0125
broadening = 0.3
W = 256
f32 = jnp.float32
b16 = jnp.bfloat16
VMEM_BYTES = 32 * 2**20


def dot_nt(left, right):
    return lax.dot_general(left, right, (((1,), (1,)), ((), ())), preferred_element_type=f32)


def dot_nn(left, right):
    return lax.dot_general(left, right, (((1,), (0,)), ((), ())), preferred_element_type=f32)


def split(value):
    high = value.astype(b16)
    return high, (value - high.astype(f32)).astype(b16)


def dot3(left, right, dot=dot_nt):
    return dot(left[0], right[0]) + (dot(left[1], right[0]) + dot(left[0], right[1]))


def cdot3(left, right, dot=dot_nt):
    (lr, li), (rr, ri) = left, right
    first = dot3(split(lr), split(rr), dot)
    second = dot3(split(li), split(ri), dot)
    summed = dot3(split(lr + li), split(rr + ri), dot)
    return first - second, summed - first - second


def eye_mask():
    rows = lax.broadcasted_iota(jnp.int32, (W, W), 0)
    columns = lax.broadcasted_iota(jnp.int32, (W, W), 1)
    return rows == columns


def diagonal_row(value):
    return jnp.sum(jnp.where(eye_mask(), value, 0.0), axis=0, keepdims=True)


def diagonal_and_rest(energy, onsite, sr, si):
    br = -(onsite + sr)
    bi = -si
    dr = energy + diagonal_row(br)
    di = broadening + diagonal_row(bi)
    scale = 1.0 / (dr * dr + di * di)
    dr, di = dr * scale, -di * scale
    mask = eye_mask()
    br = jnp.where(mask, 0.0, br)
    bi = jnp.where(mask, 0.0, bi)
    return br, bi, dr, di, br * dr - bi * di, br * di + bi * dr


def chain_step(energy, onsite, lead, sr, si):
    _, _, dr, di, fr, fi = diagonal_and_rest(energy, onsite, sr, si)
    frh, fih = fr.astype(b16), fi.astype(b16)
    leads = jnp.concatenate(split(lead), axis=0)
    pr, pi = dot_nt(leads, frh), dot_nt(leads, fih)
    pr, pi = pr[:W] + pr[W:], pi[:W] + pi[W:]
    prh, pih = pr.astype(b16), pi.astype(b16)
    qr = dot_nt(prh, frh) - dot_nt(pih, fih)
    qi = dot_nt(prh, fih) + dot_nt(pih, frh)
    x = lead - pr
    xr, xi = x * dr + pi * di, x * di - pi * dr
    return cdot3((xr, xi), (lead + qr, qi))


def spectral_row(energy, onsite, sr, si):
    br, bi, dr, di, fr, fi = diagonal_and_rest(energy, onsite, sr, si)
    frh, fih, brh, bih = (v.astype(b16) for v in (fr, fi, br, bi))
    yr = br - (dot_nt(frh, brh) - dot_nt(fih, bih))
    yi = bi - (dot_nt(frh, bih) + dot_nt(fih, brh))
    tr = jnp.sum(fr * yr - fi * yi, axis=1, keepdims=True)
    ti = jnp.sum(fr * yi + fi * yr, axis=1, keepdims=True)
    tr = diagonal_row(jnp.broadcast_to(tr, (W, W)))
    ti = diagonal_row(jnp.broadcast_to(ti, (W, W)))
    return -2.0 * (di + (dr * dr - di * di) * ti + 2.0 * dr * di * tr)


def crossing_row(energy, onsite, s0, s1, r0, r1):
    br, bi, dr, di, fr, fi = diagonal_and_rest(energy, onsite, s0 + r0, s1 + r1)
    f2r, f2i = cdot3((fr, fi), (fr, fi), dot_nn)
    f3r, f3i = cdot3((f2r, f2i), (fr, fi), dot_nn)
    one = jnp.where(eye_mask(), 1.0, 0.0)
    kr, ki = one - fr + f2r - f3r, -fi + f2i - f3i
    dcol_r = jnp.where(eye_mask(), dr, 0.0)
    dcol_i = jnp.where(eye_mask(), di, 0.0)
    dcol_r = jnp.sum(dcol_r, axis=1, keepdims=True)
    dcol_i = jnp.sum(dcol_i, axis=1, keepdims=True)
    gr, gi = dcol_r * kr - dcol_i * ki, dcol_r * ki + dcol_i * kr
    left, right = split(-2.0 * s1), split(-2.0 * r1)
    grs, gis = split(gr), split(gi)
    ar, ai = dot3(left, grs, dot_nn), dot3(left, gis, dot_nn)
    cr, ci = dot3(grs, right, dot_nt), dot3(gis, right, dot_nt)
    return jnp.sum(ar * cr + ai * ci, axis=0, keepdims=True)


H2 = W // 2


def here(name):
    if name == "x":
        return 2 * lax.axis_index("pair") + lax.axis_index("row")
    return lax.axis_index(name)


def on_task():
    x = here("x")
    return ((x == 0) | (x == 3)) == (here("core") == 0)


def is_outer():
    return (here("x") < 2) == (here("half") == 0)


def pack(sr, si, extra=0.0):
    rows = lax.broadcasted_iota(jnp.int32, (H2, H2), 0)
    columns = lax.broadcasted_iota(jnp.int32, (H2, H2), 1)

    def folded(value):
        low = value[H2:, H2:]
        fold = jnp.where(rows <= columns, value[:H2, :H2], low)
        diagonal = jnp.sum(jnp.where(rows == columns, low, 0.0), axis=0, keepdims=True)
        return jnp.concatenate([value[:H2, H2:], fold], axis=1), diagonal

    top, diagonal_top = folded(sr)
    bottom, diagonal_bottom = folded(si)
    row = jnp.broadcast_to(jnp.concatenate([diagonal_top, diagonal_bottom], axis=1), (8, W))
    last = jnp.where(lax.broadcasted_iota(jnp.int32, (8, W), 0) == 0, row, extra)
    return jnp.concatenate([top, bottom, last], axis=0)


def unpack(packed):
    rows = lax.broadcasted_iota(jnp.int32, (H2, H2), 0)
    columns = lax.broadcasted_iota(jnp.int32, (H2, H2), 1)

    def unfolded(value, diagonal):
        corner, fold = value[:, :H2], value[:, H2:]
        turned = fold.T
        first = jnp.where(rows <= columns, fold, turned)
        last = jnp.where(rows > columns, fold, jnp.where(rows < columns, turned, diagonal))
        top = jnp.concatenate([first, corner], axis=1)
        return jnp.concatenate([top, jnp.concatenate([corner.T, last], axis=1)], axis=0)

    return (
        unfolded(packed[:H2], packed[2 * H2 : 2 * H2 + 1, :H2]),
        unfolded(packed[H2 : 2 * H2], packed[2 * H2 : 2 * H2 + 1, H2:]),
    )


def prepare_kernel(pattern, onsite, coupling, both, mine):
    tiles = lax.broadcasted_iota(jnp.int32, (1, W), 1) // 64
    both[0] = onsite[...]
    for p in range(4):
        row = jnp.zeros((1, W), f32)
        for q in range(4):
            row = jnp.where(tiles == q, pattern[p, q].astype(f32), row)
        part = pl.ds(64 * p, 64)
        both[1, part, :] = coupling[part, :] * row
    mine[...] = both[here("core")]


def energy_of(index):
    return energy_floor + energy_spacing * index[here("y")].astype(f32)


STEPS = ((0, 7), (7, 8), (8, 16))
OUTWARD = ((1, 5), (5, 8), (8, 16))


def kept_at(t):
    part = next(k for k, (first, stop) in enumerate(STEPS) if first <= t < stop)
    return part, t - STEPS[part][0]


def sweep_kernel(part, *refs):
    first, stop = STEPS[part]
    count = stop - first
    refs = list(refs)
    index = refs.pop(0)
    start = refs.pop(0)
    both, own_onsite, own_links, near_mine, near_sent = (refs.pop(0) for _ in range(5))
    bridge = refs.pop(0) if part else None
    wire_h, wire_m, store, last = (refs.pop(0) for _ in range(4))
    hbuf, mbuf, sbuf, in_sem, out_sem = refs
    half, y, core = here("half"), here("y"), here("core")
    energy = energy_of(index)

    def start_from(chunk, column, kind, target, sem):
        away = lax.rem(column - y + 4, 4)
        own_row = core == (0 if chunk in (0, 3) else 1)

        @pl.when(own_row & (away == 0))
        def _():
            pltpu.make_async_copy(both.at[kind], target, sem).start()

        @pl.when(own_row & (away != 0))
        def _():
            source = (own_onsite, own_links)[kind].at[jnp.maximum(away - 1, 0)]
            pltpu.make_async_copy(source, target, sem).start()

        for here_too, near in ((core == kind, near_mine), (core != kind, near_sent)):

            @pl.when(~own_row & here_too)
            def _():
                pltpu.make_async_copy(near.at[away], target, sem).start()

    @pl.when(on_task() & (is_outer() if part < 2 else ~is_outer()))
    def _():
        for n in range(count):
            t = first + n
            start_from(t // 4, jnp.where(half == 0, t % 4, 3 - t % 4), 0, hbuf.at[n], in_sem.at[n, 0])
            if t % 4 < 3:
                start_from(t // 4, jnp.where(half == 0, t % 4, 2 - t % 4), 1, mbuf.at[n], in_sem.at[n, 1])
            else:

                @pl.when(half == 0)
                def _():
                    start_from(t // 4, 3, 1, mbuf.at[n], in_sem.at[n, 1])

                @pl.when(half != 0)
                def _():
                    if t % 8 == 7:
                        pltpu.make_async_copy(bridge, mbuf.at[n], in_sem.at[n, 1]).start()
                    else:
                        start_from(t // 4 + 1, 3, 1, mbuf.at[n], in_sem.at[n, 1])

        if part == 0:
            sbuf[0, 0] = jnp.zeros((W, W), f32)
            sbuf[0, 1] = jnp.where(eye_mask(), -0.5 * start[pl.ds(half, 1), :], 0.0)
        elif part == 1:
            sbuf[0] = start[...]
        else:
            sbuf[0, 0], sbuf[0, 1] = unpack(start[...])

        def kept(n):
            return (
                pltpu.make_async_copy(hbuf.at[n], wire_h.at[n], out_sem.at[n, 0]),
                pltpu.make_async_copy(mbuf.at[n], wire_m.at[n], out_sem.at[n, 1]),
                pltpu.make_async_copy(sbuf.at[n], store.at[n], out_sem.at[n, 2]),
            )

        def one(n, unused):
            pltpu.make_async_copy(wire_h.at[n], hbuf.at[n], in_sem.at[n, 0]).wait()
            pltpu.make_async_copy(wire_m.at[n], mbuf.at[n], in_sem.at[n, 1]).wait()
            for copy in kept(n):
                copy.start()
            m = mbuf[n]
            lead = jnp.where(half == 0, m.T, m)
            nr, ni = chain_step(energy, hbuf[n], lead, sbuf[n, 0], sbuf[n, 1])
            sbuf[n + 1, 0] = nr
            sbuf[n + 1, 1] = ni
            return 0

        lax.fori_loop(0, count, one, 0)
        if part:
            last[...] = pack(sbuf[count, 0], sbuf[count, 1])
        else:
            last[...] = sbuf[count]
        for n in range(count):
            for copy in kept(n):
                copy.wait()


def middle_kernel(index, arrived, wire_h, wire_m, store, carried, crossing, hbuf, mbuf, sbuf, in_sem):
    half = here("half")
    energy = energy_of(index)
    crossing[...] = jnp.zeros((8, W), f32)

    @pl.when(on_task() & ~is_outer())
    def _():
        copies = (
            pltpu.make_async_copy(wire_h.at[kept_at(15)[1]], hbuf, in_sem.at[0]),
            pltpu.make_async_copy(wire_m.at[kept_at(14)[1]], mbuf, in_sem.at[1]),
            pltpu.make_async_copy(store.at[kept_at(15)[1]], sbuf, in_sem.at[2]),
        )
        for copy in copies:
            copy.start()
        sr, si = unpack(arrived[...])
        for copy in copies:
            copy.wait()

        @pl.when(half != 0)
        def _():
            row = crossing_row(energy, hbuf[...], sr, si, sbuf[0], sbuf[1])
            crossing[...] = jnp.broadcast_to(jnp.sum(row, axis=1, keepdims=True), (8, W))

        m = mbuf[...]
        lead = jnp.where(half == 0, m, m.T)
        nr, ni = chain_step(energy, hbuf[...], lead, sr, si)
        carried[0] = nr
        carried[1] = ni


def inner_kernel(leg, places, *refs):
    first, stop = OUTWARD[leg]
    count = stop - first
    refs = list(refs)
    index = refs.pop(0)
    start = refs.pop(0)
    totals = [refs.pop(0) for _ in range(2)] if leg else None
    links = [refs.pop(0) for _ in range(3)] if leg else None
    kept = {place: refs.pop(0) for place in places}
    leaving, entered, hbuf, mbuf, carried, in_sem, out_sem = refs
    half = here("half")
    energy = energy_of(index)

    @pl.when(on_task() & ~is_outer())
    def _():
        for n in range(count):
            t = first + n
            k, at_n = kept_at(15 - t)
            pltpu.make_async_copy(kept[0, k].at[at_n], hbuf.at[n], in_sem.at[n, 0]).start()
            if t == 7:
                away = lax.rem(7 - here("y"), 4)
                upper, brings = half != 0, here("core") != 0
                for wanted, source in (
                    (~upper, links[0]),
                    (upper & brings, links[1]),
                    (upper & ~brings, links[2].at[away]),
                ):

                    @pl.when(wanted)
                    def _():
                        pltpu.make_async_copy(source, mbuf.at[n], in_sem.at[n, 1]).start()

            else:
                k, at_n = kept_at(14 - t)
                pltpu.make_async_copy(kept[1, k].at[at_n], mbuf.at[n], in_sem.at[n, 1]).start()
        carried[0] = start[...]

        def one(n, unused):
            pltpu.make_async_copy(hbuf.at[n], hbuf.at[n], in_sem.at[n, 0]).wait()
            pltpu.make_async_copy(mbuf.at[n], mbuf.at[n], in_sem.at[n, 1]).wait()
            pltpu.make_async_copy(carried.at[n], entered.at[n], out_sem.at[n]).start()
            m = mbuf[n]
            lead = jnp.where(half == 0, m, m.T)
            nr, ni = chain_step(energy, hbuf[n], lead, carried[n, 0], carried[n, 1])
            carried[n + 1, 0] = nr
            carried[n + 1, 1] = ni
            return 0

        lax.fori_loop(0, count, one, 0)
        if leg:
            leaving[...] = pack(carried[count, 0], carried[count, 1], totals[0][...] + totals[1][...])
        else:
            leaving[...] = carried[count]
        for n in range(count):
            pltpu.make_async_copy(carried.at[n], entered.at[n], out_sem.at[n]).wait()


def last_kernel(places, *refs):
    first, stop = OUTWARD[2]
    count = stop - first
    refs = list(refs)
    index, start, middle_start, own_total, sent_total = (refs.pop(0) for _ in range(5))
    entered = [refs.pop(0) for _ in range(2)]
    kept = {place: refs.pop(0) for place in places}
    out, hbuf, mbuf, sbuf, rbuf, spectra, in_sem = refs
    half = here("half")
    energy = energy_of(index)

    def landed(n, kinds):
        for kind in kinds:
            buffer = (hbuf, mbuf, sbuf, rbuf)[kind].at[n]
            pltpu.make_async_copy(buffer, buffer, in_sem.at[n, kind]).wait()

    def spectrum(n, t, rr, ri):
        row = spectral_row(energy, hbuf[n], sbuf[n, 0] + rr, sbuf[n, 1] + ri)
        spectra[pl.ds(jnp.where(half == 0, 15 - t, t), 1)] = row[None]

    @pl.when(on_task() & is_outer())
    def _():
        for n in range(count):
            t = first + n
            k, at_n = kept_at(15 - t)
            pltpu.make_async_copy(kept[0, k].at[at_n], hbuf.at[n], in_sem.at[n, 0]).start()
            pltpu.make_async_copy(kept[2, k].at[at_n], sbuf.at[n], in_sem.at[n, 2]).start()
            if t < 15:
                k, at_n = kept_at(14 - t)
                pltpu.make_async_copy(kept[1, k].at[at_n], mbuf.at[n], in_sem.at[n, 1]).start()
        carried = rbuf.at[0]
        carried[0], carried[1] = unpack(start[...])

        def one(n, unused):
            landed(n, (0, 1, 2))
            spectrum(n, first + n, carried[0], carried[1])
            m = mbuf[n]
            lead = jnp.where(half == 0, m, m.T)
            nr, ni = chain_step(energy, hbuf[n], lead, carried[0], carried[1])
            carried[0] = nr
            carried[1] = ni
            return 0

        lax.fori_loop(0, count - 1, one, 0)
        landed(count - 1, (0, 2))
        spectrum(count - 1, stop - 1, carried[0], carried[1])

    @pl.when(on_task() & ~is_outer())
    def _():
        for t in range(8):
            k, at_n = kept_at(15 - t)
            pltpu.make_async_copy(kept[0, k].at[at_n], hbuf.at[t], in_sem.at[t, 0]).start()
            pltpu.make_async_copy(kept[2, k].at[at_n], sbuf.at[t], in_sem.at[t, 2]).start()
            if t:
                leg = 0 if t < OUTWARD[1][0] else 1
                source = entered[leg].at[t - OUTWARD[leg][0]]
                pltpu.make_async_copy(source, rbuf.at[t], in_sem.at[t, 3]).start()
        rbuf[0, 0], rbuf[0, 1] = unpack(middle_start[...])
        landed(0, (0, 2))
        spectrum(0, 0, rbuf[0, 0], rbuf[0, 1])

        def one(t, unused):
            landed(t, (0, 2, 3))
            spectrum(t, t, rbuf[t, 0], rbuf[t, 1])
            return 0

        lax.fori_loop(1, 8, one, 0)

    @pl.when(on_task())
    def _():
        outer_total = start[pl.ds(2 * H2, 8), :]
        total = jnp.where(is_outer(), outer_total, own_total[...] + sent_total[...])
        base = 8 * lax.axis_index("pair")
        for place in range(8):
            out[place, pl.ds(0, 1), :] = spectra[base + place]
            out[place, pl.ds(1, 7), :] = total[1:8]


def deal_kernel(pieces, spectral, totals):
    row = jnp.where(lax.axis_index("pair") == 0, here("core"), 1 - here("core"))
    for e in range(4):
        spectral[pl.ds(e, 1), :] = pieces[4 * row + e, pl.ds(0, 1), :]
        totals[e] = jnp.max(pieces[4 * row + e, pl.ds(1, 1), :])


def vmem():
    return pl.BlockSpec(memory_space=pltpu.VMEM)


def smem():
    return pl.BlockSpec(memory_space=pltpu.SMEM)


def anywhere():
    return pl.BlockSpec(memory_space=pl.ANY)


def shape(*sizes):
    return jax.ShapeDtypeStruct(sizes, f32)


def params():
    return pltpu.CompilerParams(vmem_limit_bytes=VMEM_BYTES)


def cost(steps):
    return pl.CostEstimate(flops=int(steps * 1.4e9), bytes_accessed=int(steps * 2**20), transcendentals=0)


def prepare(pattern, onsite, coupling):
    return pl.pallas_call(
        prepare_kernel,
        out_shape=(shape(2, W, W), shape(W, W)),
        in_specs=[smem(), vmem(), vmem()],
        out_specs=[vmem(), vmem()],
        name="prepare",
    )(pattern, onsite, coupling)


def sweep(part, index, start, sets, bridge=None):
    first, stop = STEPS[part]
    count = stop - first
    arrays = list(sets)
    if bridge is not None:
        arrays.append(bridge)
    outs = [shape(count, W, W), shape(count, W, W), shape(count, 2, W, W)]
    outs.append(shape(2 * H2 + 8, W) if part else shape(2, W, W))
    specs = [anywhere(), anywhere(), anywhere(), vmem()]
    scratch = [
        pltpu.VMEM((count, W, W), f32),
        pltpu.VMEM((count, W, W), f32),
        pltpu.VMEM((count + 1, 2, W, W), f32),
        pltpu.SemaphoreType.DMA((count, 2)),
        pltpu.SemaphoreType.DMA((count, 3)),
    ]
    return pl.pallas_call(
        functools.partial(sweep_kernel, part),
        out_shape=tuple(outs),
        in_specs=[smem(), vmem()] + [anywhere()] * len(arrays),
        out_specs=specs,
        scratch_shapes=scratch,
        name="sweep_%d" % part,
        compiler_params=params(),
        cost_estimate=cost(count),
    )(index, start, *arrays)


def middle(index, arrived, wire_h, wire_m, store):
    return pl.pallas_call(
        middle_kernel,
        out_shape=(shape(2, W, W), shape(8, W)),
        in_specs=[smem(), vmem(), anywhere(), anywhere(), anywhere()],
        out_specs=[vmem()] * 2,
        scratch_shapes=[
            pltpu.VMEM((W, W), f32),
            pltpu.VMEM((W, W), f32),
            pltpu.VMEM((2, W, W), f32),
            pltpu.SemaphoreType.DMA((3,)),
        ],
        name="middle",
        compiler_params=params(),
        cost_estimate=cost(2),
    )(index, arrived, wire_h, wire_m, store)


def inner_leg(leg, index, start, totals, links, kept):
    first, stop = OUTWARD[leg]
    count = stop - first
    places = set()
    for t in range(first, stop):
        places.add((0, kept_at(15 - t)[0]))
        if t != 7:
            places.add((1, kept_at(14 - t)[0]))
    places = sorted(places)
    arrays = [*links, *(kept[k][kind] for kind, k in places)]
    return pl.pallas_call(
        functools.partial(inner_kernel, leg, places),
        out_shape=(shape(2 * H2 + 8, W) if leg else shape(2, W, W), shape(count, 2, W, W)),
        in_specs=[smem()] + [vmem()] * (1 + len(totals)) + [anywhere()] * len(arrays),
        out_specs=[vmem(), anywhere()],
        scratch_shapes=[
            pltpu.VMEM((count, W, W), f32),
            pltpu.VMEM((count, W, W), f32),
            pltpu.VMEM((count + 1, 2, W, W), f32),
            pltpu.SemaphoreType.DMA((count, 2)),
            pltpu.SemaphoreType.DMA((count,)),
        ],
        name="outward_%d" % leg,
        compiler_params=params(),
        cost_estimate=cost(count),
    )(index, start, *totals, *arrays)


def last_leg(index, start, middle_start, totals, entered, kept):
    first, stop = OUTWARD[2]
    count = stop - first
    places = [(kind, k) for kind in (0, 2) for k in range(3)] + [(1, 0)]
    arrays = [*entered, *(kept[k][kind] for kind, k in places)]
    return pl.pallas_call(
        functools.partial(last_kernel, places),
        out_shape=shape(8, 8, W),
        in_specs=[smem()] + [vmem()] * 4 + [anywhere()] * len(arrays),
        out_specs=vmem(),
        scratch_shapes=[
            pltpu.VMEM((count, W, W), f32),
            pltpu.VMEM((count, W, W), f32),
            pltpu.VMEM((count, 2, W, W), f32),
            pltpu.VMEM((count, 2, W, W), f32),
            pltpu.VMEM((16, 1, W), f32),
            pltpu.SemaphoreType.DMA((count, 4)),
        ],
        name="outward_2",
        compiler_params=params(),
        cost_estimate=cost(1.2 * count),
    )(index, start, middle_start, *totals, *arrays)


def deal(pieces):
    return pl.pallas_call(
        deal_kernel,
        out_shape=(shape(4, W), shape(4)),
        in_specs=[vmem()],
        out_specs=[vmem(), smem()],
        name="deal",
    )(pieces)


AXES = ("half", "pair", "row", "y", "core")


def at(half, x, y, core):
    return ((half * 4 + x) * 4 + y) * 2 + core


def moved(value, move, chosen=lambda half, x, y, core: True):
    pairs = []
    for half in range(2):
        for x in range(4):
            for y in range(4):
                for core in range(2):
                    if chosen(half, x, y, core):
                        pairs.append((at(half, x, y, core), at(*move(half, x, y, core))))
    return lax.ppermute(value, AXES, pairs)


def is_task(half, x, y, core):
    return (x in (0, 3)) == (core == 0)


def outer_task(half, x, y, core):
    return is_task(half, x, y, core) and (x < 2) == (half == 0)


def inner_task(half, x, y, core):
    return is_task(half, x, y, core) and (x < 2) != (half == 0)


def along_y(value, shift, chosen=lambda *place: True):
    return moved(value, lambda half, x, y, core: (half, x, (y + shift) % 4, core), chosen)


def to_partner(value, chosen=lambda *place: True):
    return moved(value, lambda half, x, y, core: (half, x ^ 1, y, core), chosen)


def to_next(value, chosen):
    return moved(value, lambda half, x, y, core: (half, 3 - x, y, core), chosen)


def to_other_half(value, chosen):
    return moved(value, lambda half, x, y, core: (1 - half, 3 - x, y, core), chosen)


def across(value):
    return moved(value, lambda half, x, y, core: (half, x, y, 1 - core), lambda *place: not is_task(*place))


def on_device(onsite, coupling, pattern, contact_rates, energy_index):
    both, mine = prepare(pattern[0], onsite[0], coupling[0])
    near = to_partner(mine)
    left, right = along_y(mine, 1), along_y(mine, -1)
    opposite = jnp.concatenate([along_y(left[:H2], 1), along_y(right[H2:], -1)], axis=0)
    own_row = jnp.stack([right, opposite, left])
    near_row = jnp.stack([near, along_y(near, -1), to_partner(opposite), along_y(near, 1)])
    own_sent, near_sent = across(own_row), across(near_row)
    brings_onsite = here("core") == 0
    own_onsite = jnp.where(brings_onsite, own_row, own_sent)
    own_links = jnp.where(brings_onsite, own_sent, own_row)
    sets = (both, own_onsite, own_links, near_row, near_sent)
    x, y = here("x"), here("y")
    row_links = jnp.where(lax.rem(x, 2) == 1, jnp.concatenate([mine[None], own_row], axis=0), near_row)
    link = lax.dynamic_index_in_dim(row_links, lax.rem(7 - y, 4), 0, keepdims=False)
    bridge = moved(
        link,
        lambda half, x, y, core: (half if x < 2 else 1, 3 - x, y, 0 if x in (0, 3) else 1),
        lambda half, x, y, core: core == 1 and not (half == 1 and x >= 2),
    )
    *first, carry = sweep(0, energy_index, contact_rates, sets)
    *edge, leaving = sweep(1, energy_index, carry, sets, bridge)
    arrived = to_next(leaving, outer_task)
    *inner, leaving = sweep(2, energy_index, arrived, sets, bridge)
    kept = [first, edge, inner]
    crossed = to_other_half(leaving, inner_task)
    carry, total = middle(energy_index, crossed, *inner)
    sent_total = to_other_half(
        total, lambda half, x, y, core: half == 1 and inner_task(half, x, y, core)
    )
    totals = [total, sent_total]
    carry, *entered = inner_leg(0, energy_index, carry, [], [], kept)
    leaving, later = inner_leg(1, energy_index, carry, totals, [bridge, link, near_sent], kept)
    entered.append(later)
    arrived = to_next(leaving, inner_task)
    pieces = last_leg(energy_index, arrived, crossed, totals, entered, kept)
    pieces = lax.all_to_all(pieces, ("row", "y"), 0, 0)
    spectral, totals = deal(pieces)
    return spectral[None], totals


def solution(mesh):
    fine = Mesh(mesh.devices.reshape(2, 2, 2, 4, 2, 2), ("half", "pair", "row", "y", "plane", "core"))
    slab = ("half", "pair", "row", "y")
    part = ("plane", "core")
    return jax.shard_map(
        on_device,
        mesh=fine,
        in_specs=(P(slab), P(slab), P(slab), P(), P(part)),
        out_specs=(P(slab, part, None), P(part)),
        check_vma=False,
    )
```
